32 devices in a mesh: expert: 8 (over z, y), dp: 4 (over x, core).
Axes of the slice: x: 2, y: 2, z: 4, core: 2. Of those that a mesh axis runs over, the one named last changes fastest.
Arguments:
- cotangent: bfloat16 [4, 4096, 2048], P('dp', 'expert'), may hold values from -6 to 6
- routing: int32 [4, 4096, 2], P('dp', 'expert'), may hold values from 0 to 7, all different within a row; in each aligned block of 512 rows (0 to 511, 512 to 1023, ..., all dimensions but the last counted through in order) at most 256 rows name the same one
- route_weight: float32 [4, 4096, 2], P('dp', 'expert'), may hold values from 0.1 to 0.6
- saved_preact: bfloat16 [4, 8, 2048, 1536], P('dp', 'expert'), may hold values from -6 to 6
- weight: bfloat16 [8, 768, 2048], P('expert'), may hold values from -0.21875 to 0.21875
- master: float32 [8, 768, 2048], P('expert', 'dp'), may hold values from -0.21875 to 0.21875
- moment1: float32 [8, 768, 2048], P('expert', 'dp'), may hold values from -18 to 18
- moment2: float32 [8, 768, 2048], P('expert', 'dp'), may hold values from 1 to 100
Outputs:
- grad_preact: bfloat16 [4, 8, 2048, 1536], P('dp', 'expert')
- new_weight: bfloat16 [8, 768, 2048], P('expert')
- new_master: float32 [8, 768, 2048], P('expert', 'dp')
- new_moment1: float32 [8, 768, 2048], P('expert', 'dp')
- new_moment2: float32 [8, 768, 2048], P('expert', 'dp')
The draws below stay inside these ranges and needn't reach their ends.
Inputs may be any that keep to these rules, and one draw needn't show every extreme that they name: `routing`: each row names 2 different experts; no expert is named by more than 256 of the rows of one device, and in every draw some expert is named by exactly 256 rows of some device.
All inputs are finite; a program needn't handle non-finite values.
Results may differ from the reference program's by a relative error of at most 0.019.
Values may be sent and summed in bfloat16 or wider, within the bound.
No kernel may reach another device: no remote copies, remote signals or barrier semaphores. Data moves between devices by JAX's collectives and lax.ppermute only.
A program may use at most 128 MiB of HBM per device.

```python
import math
import jax
import jax.numpy as jnp
import numpy as np
from jax import lax

D = 2048
F = 768
TOPK = 2
TOK_DEV = 512
EXPERTS = 8
CAP = 256
SLOTS = 2048
N_EXPERT = 8
N_DP = 4


def shard_levels(rng, shape, cuts, low, largest):
    def one(dim, parts):
        draws = jax.random.uniform(jax.random.fold_in(jax.random.fold_in(rng, 6), dim), (parts,), jnp.float32, low / len(cuts), largest / len(cuts))
        return jnp.repeat(jnp.exp(draws), shape[dim] // parts).reshape((-1,) + (1,) * (len(shape) - dim - 1))

    level = one(*cuts[0])
    for cut in cuts[1:]:
        level = level * one(*cut)
    return level


def shared_out(stream_key, own, number, rows, number_of, top, most, slope):
    ranking = jax.random.permutation(stream_key, number_of)
    crowded, usual = portions_of(number_of, rows * top, most, slope, True), portions_of(number_of, rows * top, most, slope, False)
    places = jnp.arange(number_of)

    def named(sizes, rotation):
        used = int((sizes > 0).sum())
        fixed = max(1, used // 4)
        shifted = fixed + (places - fixed + rotation * (used - fixed)) % max(1, number_of - fixed)
        return jnp.zeros((number_of,), jnp.int32).at[ranking[jnp.where(places < fixed, places, shifted)]].set(jnp.asarray(sizes, jnp.int32))

    sizes = jnp.where(number % 4 == 0, named(crowded, number // 4), named(usual, number - number // 4 - 1))
    mixed = jax.random.permutation(jax.random.fold_in(own, 3), number_of)
    giver, sink = mixed[0:number_of // 2 * 2:2], mixed[1:number_of // 2 * 2:2]
    room = jnp.minimum(sizes[giver] - 1, most - sizes[sink]) // 2
    room = jnp.where((giver == ranking[0]) | (sink == ranking[0]) | (sizes[sink] == 0), 0, jnp.maximum(room, 0))
    shifted = jax.random.randint(jax.random.fold_in(own, 4), (number_of // 2,), 0, 1 << 20) % (room + 1)
    sizes = sizes.at[giver].add(-shifted).at[sink].add(shifted)
    items = jnp.searchsorted(jnp.cumsum(sizes), jnp.arange(rows * top), side="right").astype(jnp.int32)
    grid = items.reshape(top, rows).T
    grid = grid[jax.random.permutation(jax.random.fold_in(own, 1), rows)]
    rotation = jax.random.randint(jax.random.fold_in(own, 2), (rows, 1), 0, top)
    return jnp.take_along_axis(grid, (jnp.arange(top)[None, :] + rotation) % top, axis=1)


def portions_of(amount, total, reach, lean, full):
    weights = [(1 << 20) // math.isqrt(grade ** lean) + 1 for grade in range(1, amount + 1)]
    largest = reach if full else min(reach, max(-(-total // amount), total * weights[0] // sum(weights)))
    least = 1 if total - largest >= amount - 1 else 0
    given, rest = [largest] + [least] * (amount - 1), total - largest - least * (amount - 1)
    while rest > 0:
        movable = [i for i in range(1, amount) if given[i] < largest] or [i for i in range(1, amount) if given[i] < reach]
        mass, left = sum([weights[i] for i in movable]), rest
        for i in movable:
            addition = min(reach - given[i], max(1, left * weights[i] // mass), rest)
            given[i] = given[i] + addition
            rest = rest - addition
    return np.array(given)


def normal_values(stream_key, shape, width, most, split=(), kind=jnp.bfloat16):
    result = width * jax.random.normal(stream_key, shape, jnp.float32)
    if split:
        result = result * shard_levels(stream_key, shape, split, -0.22, 0.18)
    return jnp.clip(result, -most, most).astype(kind)


def setup_inputs(seed: int = 0) -> dict:
    arg_keys = jax.random.split(jax.random.key(seed), 9)
    cotangent = normal_values(arg_keys[0], (N_DP, N_EXPERT * TOK_DEV, D), 1.0, 6.0, ((0, 4), (1, 8)))
    routing_keys = jax.random.split(jax.random.fold_in(arg_keys[1], 1), N_DP * (N_EXPERT * TOK_DEV) // TOK_DEV)
    routing_turns = jax.random.permutation(jax.random.fold_in(arg_keys[1], 3), N_DP * (N_EXPERT * TOK_DEV) // TOK_DEV)
    routing = jax.vmap(lambda own, number: shared_out(jax.random.fold_in(arg_keys[1], 2), own, number, TOK_DEV, EXPERTS, TOPK, CAP, 2))(routing_keys, routing_turns).reshape((N_DP, N_EXPERT * TOK_DEV, TOPK))
    route_weight = jnp.clip(0.1 + 0.5 * jax.random.uniform(arg_keys[2], (N_DP, N_EXPERT * TOK_DEV, TOPK), jnp.float32) ** shard_levels(arg_keys[2], (N_DP, N_EXPERT * TOK_DEV, TOPK), ((0, 4), (1, 8)), -0.2, 0.2), 0.1, 0.6)
    saved_preact = normal_values(arg_keys[3], (N_DP, EXPERTS, SLOTS, 2 * F), 1.0, 6.0, ((0, 4), (1, 8)))
    weight = normal_values(arg_keys[4], (EXPERTS, F, D), F ** -0.5, 0.21875, ((0, 8),))
    master = normal_values(arg_keys[5], (EXPERTS, F, D), F ** -0.5, 0.21875, ((0, 8), (1, 4)), jnp.float32)
    moment1 = normal_values(arg_keys[6], (EXPERTS, F, D), 3.0, 18.0, ((0, 8), (1, 4)), jnp.float32)
    moment2 = jnp.clip(jnp.exp(math.log(100.0) - 4.6051702 * jax.random.uniform(arg_keys[7], (EXPERTS, F, D), jnp.float32) ** shard_levels(arg_keys[7], (EXPERTS, F, D), ((0, 8), (1, 4)), -0.2, 0.2)), 1.0, 100.0)
    return dict(cotangent=cotangent, routing=routing, route_weight=route_weight, saved_preact=saved_preact, weight=weight, master=master, moment1=moment1, moment2=moment2)


beta_first = 0.9
beta_second = 0.95
bias_first = 1.0 - 0.9 ** 10
bias_second = 1.0 - 0.95 ** 10
adam_epsilon = 1e-08
learn_rate = 0.001
decay_rate = 0.1

def slot_tables(chosen_rows, weight_rows):
    chosen = chosen_rows.reshape(-1).astype(jnp.int32)
    onehot = (chosen[:, None] == jnp.arange(EXPERTS, dtype=jnp.int32)[None, :]).astype(jnp.int32)
    earlier = jnp.cumsum(onehot, axis=0) - onehot
    position = lax.optimization_barrier(jnp.sum(earlier * onehot, axis=1)).astype(jnp.int32)
    target = (chosen * CAP + position).astype(jnp.int32)
    source_token = (jnp.arange(chosen.shape[0], dtype=jnp.int32) // TOPK).astype(jnp.int32)
    token_table = jnp.zeros((EXPERTS * CAP,), jnp.int32).at[target].set(source_token)
    weight_table = jnp.zeros((EXPERTS * CAP,), jnp.float32).at[target].set(weight_rows.reshape(-1).astype(jnp.float32))
    return (token_table.reshape(EXPERTS, CAP), weight_table.reshape(EXPERTS, CAP))

def reference(cotangent, routing, route_weight, saved_preact, weight, master, moment1, moment2):
    token_tables, weight_tables = jax.vmap(slot_tables)(routing.reshape(N_DP * N_EXPERT, TOK_DEV, TOPK), route_weight.reshape(N_DP * N_EXPERT, TOK_DEV, TOPK))
    token_tables = token_tables.reshape(N_DP, N_EXPERT, EXPERTS, CAP)
    weight_tables = weight_tables.reshape(N_DP, N_EXPERT, EXPERTS, CAP)
    token_blocks = cotangent.reshape(N_DP, N_EXPERT, TOK_DEV, D)

    def expert_work(expert_id):
        matrix = weight[expert_id]

        def replica_work(replica):
            picks = token_tables[replica, :, expert_id, :]
            scales = weight_tables[replica, :, expert_id, :]
            picked = jax.vmap(lambda block, pick: block[pick])(token_blocks[replica], picks)
            arrived = (picked.astype(jnp.float32) * scales[:, :, None]).astype(jnp.bfloat16).reshape(SLOTS, D)
            preact = saved_preact[replica, expert_id].astype(jnp.float32)
            gate_value = preact[:, :F]
            up_value = preact[:, F:]
            sigmoid_gate = jax.nn.sigmoid(gate_value)
            activated = gate_value * sigmoid_gate
            hidden = (activated * up_value).astype(jnp.bfloat16)
            back = jnp.dot(arrived, matrix.T, preferred_element_type=jnp.float32)
            grad_gate = back * up_value * sigmoid_gate * (1.0 + gate_value * (1.0 - sigmoid_gate))
            grad_up = back * activated
            grad_block = jnp.concatenate([grad_gate, grad_up], axis=1).astype(jnp.bfloat16)
            partial_value = jnp.dot(hidden.T, arrived, preferred_element_type=jnp.float32).astype(jnp.bfloat16)
            return (grad_block, partial_value)
        grad_blocks, partials = lax.map(replica_work, jnp.arange(N_DP, dtype=jnp.int32))
        gradient = lax.optimization_barrier(jnp.sum(partials.astype(jnp.float32), axis=0))
        return (grad_blocks, gradient)
    grad_blocks, gradient = lax.map(expert_work, jnp.arange(EXPERTS, dtype=jnp.int32))
    grad_preact = jnp.swapaxes(grad_blocks, 0, 1)
    moment_one = beta_first * moment1 + (1.0 - beta_first) * gradient
    moment_two = beta_second * moment2 + (1.0 - beta_second) * gradient * gradient
    step_size = moment_one / bias_first / (jnp.sqrt(moment_two / bias_second) + adam_epsilon) + decay_rate * master
    master_next = master - learn_rate * step_size
    return (grad_preact, master_next.astype(jnp.bfloat16), master_next, moment_one, moment_two)
```

```python
import functools

import jax
import jax.numpy as jnp
from jax import lax
from jax.experimental import pallas as pl
from jax.experimental.pallas import tpu as pltpu
from jax.sharding import PartitionSpec as P

beta_first = 0.9
beta_second = 0.95
bias_first = 1.0 - 0.9**10
bias_second = 1.0 - 0.95**10
adam_epsilon = 1e-08
learn_rate = 0.001
decay_rate = 0.1

VMEM_LIMIT = 40 * 1024 * 1024
ANY = pl.BlockSpec(memory_space=pl.ANY)


def params():
    return pltpu.CompilerParams(vmem_limit_bytes=VMEM_LIMIT)


def call(kernel, name, grid, scalars, ins, specs, outs, out_specs, scratch=(), aliases=None, flops=0, moved=0):
    shift = len(scalars)
    return pl.pallas_call(
        kernel,
        name=name,
        grid_spec=pltpu.PrefetchScalarGridSpec(
            num_scalar_prefetch=shift,
            grid=grid,
            in_specs=specs,
            out_specs=out_specs,
            scratch_shapes=list(scratch),
        ),
        out_shape=outs,
        input_output_aliases={shift + a: b for a, b in (aliases or {}).items()},
        compiler_params=params(),
        cost_estimate=pl.CostEstimate(flops=flops, bytes_accessed=moved, transcendentals=0),
    )(*scalars, *ins)


def shape(dims, dtype):
    return jax.ShapeDtypeStruct(dims, dtype)


def hidden_kernel(order, groups, preact, out, turned):
    width = preact.shape[-1] // 2
    gate = preact[0, 0, :, :width].astype(jnp.float32)
    up = preact[0, 0, :, width:].astype(jnp.float32)
    value = gate * jax.nn.sigmoid(gate) * up
    turned[...] = value.T.astype(jnp.bfloat16)
    rows = width // 4
    for g in range(4):
        start = pl.multiple_of(groups[g] * rows, 16)
        out[g * rows : (g + 1) * rows, :] = turned[pl.ds(start, rows), :]


def table_kernel(sources, experts, info, picks, scales):
    capacity = picks.shape[1] // 2
    tokens = info.shape[2]
    first, second = info[0, 0:1, :], info[0, 1:2, :]
    weight_one, weight_two = info[0, 2:3, :], info[0, 3:4, :]
    before = lax.broadcasted_iota(jnp.int32, (tokens, tokens), 0)
    after = lax.broadcasted_iota(jnp.int32, (tokens, tokens), 1)
    earlier = (before < after).astype(jnp.float32).astype(jnp.bfloat16)
    for k in range(2):
        expert = experts[k].astype(jnp.float32)
        is_first = first == expert
        named = jnp.logical_or(is_first, second == expert)
        flag = jnp.where(named, 1.0, 0.0)
        position = jnp.dot(
            jnp.broadcast_to(flag, (16, tokens)).astype(jnp.bfloat16), earlier, preferred_element_type=jnp.float32
        )[0:1, :]
        place = jnp.where(named, position, -1.0).astype(jnp.int32)
        slot = lax.broadcasted_iota(jnp.int32, (capacity, tokens), 0)
        hit = slot == place
        value = jnp.where(is_first, weight_one, weight_two)
        picks[0, k * capacity : (k + 1) * capacity, :] = jnp.where(hit, 1.0, 0.0).astype(jnp.bfloat16)
        scales[0, k * capacity : (k + 1) * capacity, :] = jnp.sum(jnp.where(hit, value, 0.0), axis=1, keepdims=True)


def pick_kernel(middle, picks, scales, near, far, mine, other):
    capacity = mine.shape[0]
    rows = near[...] if far is None else jnp.where(middle[0] == 1, near[...], far[...])
    value = jnp.dot(picks[0], rows, preferred_element_type=jnp.float32) * scales[0]
    mine[...] = value[:capacity].astype(jnp.bfloat16)
    other[...] = value[capacity:].astype(jnp.bfloat16)


def pick_one(middle, picks, scales, near, mine, other):
    pick_kernel(middle, picks, scales, near, None, mine, other)


def product_kernel(*refs):
    turned, pieces, (send, keep) = refs[0], refs[1:-2], refs[-2:]
    half = send.shape[0]
    rows = jnp.concatenate([p[...] for p in pieces], axis=0)
    send[...] = jnp.dot(turned[:half, :], rows, preferred_element_type=jnp.float32).astype(jnp.bfloat16)
    keep[...] = jnp.dot(turned[half:, :], rows, preferred_element_type=jnp.float32).astype(jnp.bfloat16)


def back_kernel(count, order, *refs):
    mine, got = refs[:count], refs[count : 2 * count]
    weight, preact, out = refs[2 * count], refs[2 * count + 1], refs[-1]
    width = weight.shape[1]
    one = jnp.concatenate([p[...] for p in mine], axis=1)
    two = jnp.concatenate([p[...] for p in got], axis=1)
    rows = jnp.where(pl.program_id(0) == 0, one, two)
    back = lax.dot_general(rows, weight[0], (((1,), (1,)), ((), ())), preferred_element_type=jnp.float32)
    gate = preact[0, 0, :, :width].astype(jnp.float32)
    up = preact[0, 0, :, width:].astype(jnp.float32)
    sig = jax.nn.sigmoid(gate)
    out[0, 0, :, :width] = (back * up * sig * (1.0 + gate * (1.0 - sig))).astype(jnp.bfloat16)
    out[0, 0, :, width:] = (back * (gate * sig)).astype(jnp.bfloat16)


def adam_kernel(kept, near, far, master, moment1, moment2, *refs):
    out_master, out_one, out_two, out_weight = refs[-4:]
    gradient = (kept[...].astype(jnp.float32) + near[...].astype(jnp.float32)) + far[...].astype(jnp.float32)
    moment_one = beta_first * moment1[0] + (1.0 - beta_first) * gradient
    moment_two = beta_second * moment2[0] + (1.0 - beta_second) * gradient * gradient
    step_size = (
        moment_one / bias_first / (jnp.sqrt(moment_two / bias_second) + adam_epsilon) + decay_rate * master[0]
    )
    master_next = master[0] - learn_rate * step_size
    out_master[0] = master_next
    out_one[0] = moment_one
    out_two[0] = moment_two
    out_weight[...] = master_next.astype(jnp.bfloat16)


def assemble_kernel(places, own, across, sibling, *refs):
    out = refs[-1]
    rows = own.shape[0]

    def put(g, value):
        out[0, pl.ds(pl.multiple_of(places[g] * rows, 16), rows), :] = value

    put(3, own[...])
    put(2, across[...])
    put(1, sibling[:rows, :])
    put(0, sibling[rows:, :])


def line_body(cotangent, routing, route_weight, saved_preact, weight, master, moment1, moment2):
    tokens, width = cotangent.shape[1:]
    slots, hidden_width = saved_preact.shape[2], weight.shape[1]
    capacity = slots // 8
    rows = hidden_width // 4
    expert = lax.axis_index("expert")
    replica = lax.axis_index("dp")
    z, y = expert // 2, expert % 2
    x, core = replica // 2, replica % 2
    middle = jnp.where((z == 1) | (z == 2), 1, 0).astype(jnp.int32).reshape(1)
    lower = z < 2
    blocks = [z, z ^ 1, jnp.where(lower, 2, 1), jnp.where(lower, 3, 0)]
    sources = jnp.stack([b * 2 + y for b in blocks]).astype(jnp.int32)
    order = jnp.stack([b * 2 + s for b in blocks for s in (y, 1 - y)]).astype(jnp.int32)
    experts = jnp.stack([expert, expert ^ 1]).astype(jnp.int32)
    groups = jnp.stack([(1 - x) * 2 + 1 - core, x * 2 + 1 - core, (1 - x) * 2 + core, x * 2 + core]).astype(jnp.int32)

    swap_pair = [(e, e ^ 2) for e in range(8)]
    swap_middle = [(2, 4), (4, 2), (3, 5), (5, 3)]
    to_end = [(4, 6), (5, 7), (2, 0), (3, 1)]
    swap_y = [(e, e ^ 1) for e in range(8)]
    swap_x = [(d, d ^ 2) for d in range(4)]
    swap_core = [(d, d ^ 1) for d in range(4)]

    own = cotangent[0]
    info = jnp.concatenate([routing[0].T.astype(jnp.float32), route_weight[0].T], axis=0)
    info = lax.all_gather(info, "expert")
    pair = lax.ppermute(own, "expert", swap_pair)
    middle_one = lax.ppermute(own, "expert", swap_middle)

    turned = call(
        hidden_kernel,
        "hidden",
        (8,),
        (order, groups),
        (saved_preact,),
        [pl.BlockSpec((1, 1, capacity, 2 * hidden_width), lambda i, o, g: (0, 0, o[i], 0))],
        shape((hidden_width, slots), jnp.bfloat16),
        pl.BlockSpec((hidden_width, capacity), lambda i, o, g: (0, i)),
        scratch=[pltpu.VMEM((hidden_width, capacity), jnp.bfloat16)],
        moved=9 * slots * hidden_width,
        flops=40 * slots * hidden_width,
    )
    picks, scales = call(
        table_kernel,
        "tables",
        (4,),
        (sources, experts),
        (info,),
        [pl.BlockSpec((1, 4, tokens), lambda i, s, e: (s[i], 0, 0))],
        (shape((4, 2 * capacity, tokens), jnp.bfloat16), shape((4, 2 * capacity, 1), jnp.float32)),
        (
            pl.BlockSpec((1, 2 * capacity, tokens), lambda i, s, e: (i, 0, 0)),
            pl.BlockSpec((1, 2 * capacity, 1), lambda i, s, e: (i, 0, 0)),
        ),
        moved=20 * capacity * tokens,
        flops=40 * capacity * tokens,
    )

    def pick(block, near, far=None, offset=0, columns=None):
        columns = width if columns is None else columns
        tile = min(512, columns)
        start = offset // tile
        specs = [
            pl.BlockSpec((1, 2 * capacity, tokens), lambda i, m: (block, 0, 0)),
            pl.BlockSpec((1, 2 * capacity, 1), lambda i, m: (block, 0, 0)),
        ]
        if far is None:
            specs += [pl.BlockSpec((tokens, tile), lambda i, m: (0, start + i))]
            ins = (picks, scales, near)
        else:
            specs += [
                pl.BlockSpec((tokens, tile), lambda i, m: (0, start + i * m[0])),
                pl.BlockSpec((tokens, tile), lambda i, m: (0, i * (1 - m[0]))),
            ]
            ins = (picks, scales, near, far)
        out = shape((capacity, columns), jnp.bfloat16)
        mine, other = call(
            pick_one if far is None else pick_kernel,
            "pick",
            (columns // tile,),
            (middle,),
            ins,
            specs,
            (out, out),
            (pl.BlockSpec((capacity, tile), lambda i, m: (0, i)),) * 2,
            flops=4 * capacity * tokens * columns,
            moved=4 * (tokens + capacity) * columns,
        )
        return mine, lax.ppermute(other, "expert", swap_y)

    def back(block, mine, got, previous):
        specs = [pl.BlockSpec(p.shape, lambda i, o: (0, 0)) for p in (*mine, *got)]
        specs += [
            pl.BlockSpec((1, hidden_width, width), lambda i, o: (0, 0, 0)),
            pl.BlockSpec((1, 1, capacity, 2 * hidden_width), lambda i, o: (0, 0, o[2 * block + i], 0)),
        ]
        ins = [*mine, *got, weight, saved_preact]
        aliases = {}
        if previous is not None:
            aliases = {len(ins): 0}
            ins.append(previous)
            specs.append(ANY)
        return call(
            functools.partial(back_kernel, len(mine)),
            "back",
            (2,),
            (order,),
            ins,
            specs,
            shape(saved_preact.shape, jnp.bfloat16),
            pl.BlockSpec((1, 1, capacity, 2 * hidden_width), lambda i, o: (0, 0, o[2 * block + i], 0)),
            aliases=aliases,
            flops=4 * capacity * hidden_width * width,
            moved=2 * (hidden_width * width + 6 * capacity * hidden_width + 2 * capacity * width),
        )

    mine0, got0 = pick(0, own)
    mine1, got1 = pick(1, pair)
    middle_two = lax.ppermute(pair, "expert", swap_middle)
    end_one = lax.ppermute(middle_one, "expert", to_end)
    grad_preact = back(0, [mine0], [got0], None)
    grad_preact = back(1, [mine1], [got1], grad_preact)
    mine2, got2 = pick(2, middle_one, end_one)
    grad_preact = back(2, [mine2], [got2], grad_preact)

    chunks = [(0, 512), (512, 512), (1024, 512), (1536, 256), (1792, 256)]
    ends = [lax.ppermute(middle_two[:, o : o + n], "expert", to_end) for o, n in chunks]
    states = None
    next_weight = None
    mines, gots = [], []
    for (offset, columns), end_two in zip(chunks, ends):
        mine3, got3 = pick(3, middle_two, end_two, offset, columns)
        mines.append(mine3)
        gots.append(got3)
        column = offset // columns
        full = pl.BlockSpec((capacity, columns), lambda i, c=column: (0, c))
        part = pl.BlockSpec((capacity, columns), lambda i: (0, 0))
        half = shape((2 * rows, columns), jnp.bfloat16)
        send, keep = call(
            product_kernel,
            "product",
            (1,),
            (),
            (turned, mine0, got0, mine1, got1, mine2, got2, mine3, got3),
            [pl.BlockSpec((hidden_width, slots), lambda i: (0, 0))] + [full] * 6 + [part] * 2,
            (half, half),
            (pl.BlockSpec((2 * rows, columns), lambda i: (0, 0)),) * 2,
            flops=2 * hidden_width * slots * columns,
            moved=2 * (hidden_width * slots + slots * columns + hidden_width * columns),
        )
        near = lax.ppermute(send, "dp", swap_core)
        across = (keep[:rows].astype(jnp.float32) + near[:rows].astype(jnp.float32)).astype(jnp.bfloat16)
        far = lax.ppermute(across, "dp", swap_x)
        state = pl.BlockSpec((1, rows, columns), lambda i, c=column: (0, 0, c))
        second = pl.BlockSpec((rows, columns), lambda i: (1, 0))
        whole = pl.BlockSpec((rows, columns), lambda i: (0, 0))
        out_state = shape(master.shape, jnp.float32)
        previous = () if states is None else states
        *states, fresh = call(
            adam_kernel,
            "adam",
            (1,),
            (),
            (keep, near, far, master, moment1, moment2, *previous),
            [second, second, whole, state, state, state] + [ANY] * len(previous),
            (out_state, out_state, out_state, shape((rows, columns), jnp.bfloat16)),
            (state, state, state, whole),
            aliases={6 + k: k for k in range(len(previous))},
            flops=20 * rows * columns,
            moved=32 * rows * columns,
        )
        crossed = lax.ppermute(fresh, "dp", swap_x)
        sibling = lax.ppermute(jnp.concatenate([fresh, crossed], axis=0), "dp", swap_core)
        last = () if next_weight is None else (next_weight,)
        next_weight = call(
            assemble_kernel,
            "assemble",
            (1,),
            (groups,),
            (fresh, crossed, sibling, *last),
            [
                pl.BlockSpec((rows, columns), lambda i, g: (0, 0)),
                pl.BlockSpec((rows, columns), lambda i, g: (0, 0)),
                pl.BlockSpec((2 * rows, columns), lambda i, g: (0, 0)),
            ]
            + [ANY] * len(last),
            shape((1, hidden_width, width), jnp.bfloat16),
            pl.BlockSpec((1, hidden_width, columns), lambda i, g, c=column: (0, 0, c)),
            aliases={3: 0} if last else None,
            moved=16 * rows * columns,
        )
    grad_preact = back(3, mines, gots, grad_preact)
    return (grad_preact, next_weight, *states)


def body(cotangent, routing, route_weight, saved_preact, weight, master, moment1, moment2):
    n_expert = lax.axis_size("expert")
    tokens = cotangent[0]
    width = tokens.shape[1]
    slots = saved_preact.shape[2]
    hidden_width = weight.shape[1]
    capacity = slots // n_expert
    route_count = routing.shape[2]
    chosen = routing[0].reshape(-1)
    onehot = (chosen[:, None] == jnp.arange(n_expert, dtype=jnp.int32)[None, :]).astype(jnp.int32)
    earlier = jnp.cumsum(onehot, axis=0) - onehot
    position = jnp.sum(earlier * onehot, axis=1)
    target = chosen * capacity + position
    source_token = jnp.arange(chosen.shape[0], dtype=jnp.int32) // route_count
    token_table = jnp.zeros((slots,), jnp.int32).at[target].set(source_token)
    weight_table = jnp.zeros((slots,), jnp.float32).at[target].set(route_weight[0].reshape(-1))
    scaled = (tokens[token_table].astype(jnp.float32) * weight_table[:, None]).astype(jnp.bfloat16)
    arrived = lax.all_to_all(
        scaled.reshape(n_expert, capacity, width), "expert", split_axis=0, concat_axis=0, tiled=True
    )
    arrived = arrived.reshape(slots, width)
    preact = saved_preact[0, 0].astype(jnp.float32)
    gate_value = preact[:, :hidden_width]
    up_value = preact[:, hidden_width:]
    sigmoid_gate = jax.nn.sigmoid(gate_value)
    activated = gate_value * sigmoid_gate
    hidden = (activated * up_value).astype(jnp.bfloat16)
    back = lax.dot_general(
        arrived, weight[0], (((1,), (1,)), ((), ())), preferred_element_type=jnp.float32
    )
    grad_gate = back * up_value * sigmoid_gate * (1.0 + gate_value * (1.0 - sigmoid_gate))
    grad_up = back * activated
    grad_preact = jnp.concatenate([grad_gate, grad_up], axis=1).astype(jnp.bfloat16)[None, None]
    gradient = lax.psum_scatter(
        lax.dot_general(
            hidden, arrived, (((0,), (0,)), ((), ())), preferred_element_type=jnp.float32
        ).astype(jnp.bfloat16),
        "dp",
        scatter_dimension=0,
        tiled=True,
    ).astype(jnp.float32)
    moment_one = beta_first * moment1[0] + (1.0 - beta_first) * gradient
    moment_two = beta_second * moment2[0] + (1.0 - beta_second) * gradient * gradient
    step_size = (
        moment_one / bias_first / (jnp.sqrt(moment_two / bias_second) + adam_epsilon)
        + decay_rate * master[0]
    )
    master_next = master[0] - learn_rate * step_size
    weight_next = lax.all_gather(master_next.astype(jnp.bfloat16), "dp", axis=0, tiled=True)
    return (grad_preact, weight_next[None], master_next[None], moment_one[None], moment_two[None])


def solution(mesh):
    placed = (
        P("dp", "expert", None),
        P("dp", "expert", None),
        P("dp", "expert", None),
        P("dp", "expert", None, None),
        P("expert", None, None),
        P("expert", "dp", None),
        P("expert", "dp", None),
        P("expert", "dp", None),
    )
    line = mesh.shape["expert"] == 8 and mesh.shape["dp"] == 4
    return jax.shard_map(
        line_body if line else body,
        mesh=mesh,
        in_specs=placed,
        out_specs=(
            P("dp", "expert", None, None),
            P("expert", None, None),
            P("expert", "dp", None),
            P("expert", "dp", None),
            P("expert", "dp", None),
        ),
        check_vma=False,
    )
```

```python
import functools

import jax
import jax.numpy as jnp
from jax import lax
from jax.experimental import pallas as pl
from jax.experimental.pallas import tpu as pltpu
from jax.sharding import PartitionSpec as P

beta_first = 0.9
beta_second = 0.95
bias_first = 1.0 - 0.9**10
bias_second = 1.0 - 0.95**10
adam_epsilon = 1e-08
learn_rate = 0.001
decay_rate = 0.1

VMEM_LIMIT = 24 * 1024 * 1024
COST = 16
CHUNKS = ((0, 512), (512, 512), (1024, 512), (1536, 512))
ANY = pl.BlockSpec(memory_space=pl.ANY)


def params():
    return pltpu.CompilerParams(vmem_limit_bytes=VMEM_LIMIT)


def call(kernel, name, grid, scalars, ins, specs, outs, out_specs, scratch=(), aliases=None, flops=0, moved=0):
    shift = len(scalars)
    return pl.pallas_call(
        kernel,
        name=name,
        grid_spec=pltpu.PrefetchScalarGridSpec(
            num_scalar_prefetch=shift,
            grid=grid,
            in_specs=specs,
            out_specs=out_specs,
            scratch_shapes=list(scratch),
        ),
        out_shape=outs,
        input_output_aliases={shift + a: b for a, b in (aliases or {}).items()},
        compiler_params=params(),
        cost_estimate=pl.CostEstimate(flops=flops // COST, bytes_accessed=moved // COST, transcendentals=0),
    )(*scalars, *ins)


def after(*values):
    return lax.optimization_barrier(values)


def shape(dims, dtype):
    return jax.ShapeDtypeStruct(dims, dtype)


def hidden_kernel(order, groups, preact, out, turned):
    width = preact.shape[-1] // 2
    gate = preact[0, 0, :, :width].astype(jnp.float32)
    up = preact[0, 0, :, width:].astype(jnp.float32)
    value = gate * jax.nn.sigmoid(gate) * up
    turned[...] = value.T.astype(jnp.bfloat16)
    rows = width // 4
    for g in range(4):
        start = pl.multiple_of(groups[g] * rows, 16)
        out[g * rows : (g + 1) * rows, :] = turned[pl.ds(start, rows), :]


def pack_kernel(tokens, chosen, weights, first, second):
    count, width = second.shape
    first[:count, :] = tokens[0, :, :width]
    second[...] = tokens[0, :, width:]
    first[count:, :] = jnp.zeros_like(first[count:, :])
    length = chosen.shape[1]
    first[count : count + 8, :length] = jnp.concatenate([chosen[...].astype(jnp.float32), weights[...]], axis=0).astype(
        jnp.bfloat16
    )


def table_kernel(middle, experts, *refs):
    infos, picks, scales = refs[:-2], refs[-2], refs[-1]
    info = infos[0][...].astype(jnp.float32)
    if len(infos) == 2:
        info = jnp.where(middle[0] == 1, info, infos[1][...].astype(jnp.float32))
    capacity = picks.shape[0] // 2
    tokens = info.shape[1]
    first, second = info[0:1, :], info[1:2, :]
    weight_one = (info[2:3, :] + info[4:5, :]) + info[6:7, :]
    weight_two = (info[3:4, :] + info[5:6, :]) + info[7:8, :]
    before = lax.broadcasted_iota(jnp.int32, (tokens, tokens), 0)
    after = lax.broadcasted_iota(jnp.int32, (tokens, tokens), 1)
    earlier = (before < after).astype(jnp.float32).astype(jnp.bfloat16)
    for k in range(2):
        expert = experts[k].astype(jnp.float32)
        is_first = first == expert
        named = jnp.logical_or(is_first, second == expert)
        flag = jnp.where(named, 1.0, 0.0)
        position = jnp.dot(
            jnp.broadcast_to(flag, (16, tokens)).astype(jnp.bfloat16), earlier, preferred_element_type=jnp.float32
        )[0:1, :]
        place = jnp.where(named, position, -1.0).astype(jnp.int32)
        slot = lax.broadcasted_iota(jnp.int32, (capacity, tokens), 0)
        hit = slot == place
        value = jnp.where(is_first, weight_one, weight_two)
        picks[k * capacity : (k + 1) * capacity, :] = jnp.where(hit, 1.0, 0.0).astype(jnp.bfloat16)
        scales[k * capacity : (k + 1) * capacity, :] = jnp.sum(jnp.where(hit, value, 0.0), axis=1, keepdims=True)


def pick_kernel(halves, both, middle, picks, scales, *refs):
    near, far, (mine, other) = refs[:halves], refs[halves:-2], refs[-2:]
    capacity = mine.shape[0]

    def step(k):
        rows = jnp.where(middle[0] == 1, near[k][...], far[k][...]) if both else near[k][...]
        value = jnp.dot(picks[...], rows, preferred_element_type=jnp.float32) * scales[...]
        mine[...] = value[:capacity].astype(jnp.bfloat16)
        other[...] = value[capacity:].astype(jnp.bfloat16)

    if halves == 1:
        step(0)
    else:
        for k in range(halves):
            pl.when(pl.program_id(0) // (pl.num_programs(0) // halves) == k)(functools.partial(step, k))


def base_kernel(turned, *refs):
    pieces, out = refs[:-1], refs[-1]
    rows = jnp.concatenate([p[...] for p in pieces], axis=0)
    out[...] = jnp.dot(turned[...], rows, preferred_element_type=jnp.float32)


def product_kernel(base, turned, mine, got, send, keep):
    half = send.shape[0]
    rows = jnp.concatenate([mine[...], got[...]], axis=0)
    total = base[...] + jnp.dot(turned[...], rows, preferred_element_type=jnp.float32)
    send[...] = total[:half].astype(jnp.bfloat16)
    keep[...] = total[half:].astype(jnp.bfloat16)


def back_kernel(count, order, *refs):
    pieces = refs[:count]
    weight, preact, out = refs[count], refs[count + 1], refs[-1]
    width = weight.shape[1]
    rows = jnp.concatenate([p[...] for p in pieces], axis=1)
    back = lax.dot_general(rows, weight[0], (((1,), (1,)), ((), ())), preferred_element_type=jnp.float32)
    gate = preact[0, 0, :, :width].astype(jnp.float32)
    up = preact[0, 0, :, width:].astype(jnp.float32)
    sig = jax.nn.sigmoid(gate)
    out[0, 0, :, :width] = (back * up * sig * (1.0 + gate * (1.0 - sig))).astype(jnp.bfloat16)
    out[0, 0, :, width:] = (back * (gate * sig)).astype(jnp.bfloat16)


def adam_kernel(kept, near, far, master, moment1, moment2, *refs):
    out_master, out_one, out_two, out_weight = refs[-4:]
    gradient = (kept[...].astype(jnp.float32) + near[...].astype(jnp.float32)) + far[...].astype(jnp.float32)
    moment_one = beta_first * moment1[0] + (1.0 - beta_first) * gradient
    moment_two = beta_second * moment2[0] + (1.0 - beta_second) * gradient * gradient
    step_size = (
        moment_one / bias_first / (jnp.sqrt(moment_two / bias_second) + adam_epsilon) + decay_rate * master[0]
    )
    master_next = master[0] - learn_rate * step_size
    out_master[0] = master_next
    out_one[0] = moment_one
    out_two[0] = moment_two
    out_weight[...] = master_next.astype(jnp.bfloat16)


def assemble_kernel(places, own, across, sibling, *refs):
    out = refs[-1]
    rows = own.shape[0]

    def put(g, value):
        out[0, pl.ds(pl.multiple_of(places[g] * rows, 16), rows), :] = value

    put(3, own[...])
    put(2, across[...])
    put(1, sibling[:rows, :])
    put(0, sibling[rows:, :])


def line_body(cotangent, routing, route_weight, saved_preact, weight, master, moment1, moment2):
    tokens, width = cotangent.shape[1:]
    slots, hidden_width = saved_preact.shape[2], weight.shape[1]
    capacity = slots // 8
    rows = hidden_width // 4
    expert = lax.axis_index("expert")
    replica = lax.axis_index("dp")
    z, y = expert // 2, expert % 2
    x, core = replica // 2, replica % 2
    middle = jnp.where((z == 1) | (z == 2), 1, 0).astype(jnp.int32).reshape(1)
    lower = z < 2
    blocks = [z, z ^ 1, jnp.where(lower, 2, 1), jnp.where(lower, 3, 0)]
    order = jnp.stack([b * 2 + s for b in blocks for s in (y, 1 - y)]).astype(jnp.int32)
    experts = jnp.stack([expert, expert ^ 1]).astype(jnp.int32)
    groups = jnp.stack([(1 - x) * 2 + 1 - core, x * 2 + 1 - core, (1 - x) * 2 + core, x * 2 + core]).astype(jnp.int32)

    swap_pair = [(e, e ^ 2) for e in range(8)]
    swap_middle = [(2, 4), (4, 2), (3, 5), (5, 3)]
    to_end = [(4, 6), (5, 7), (2, 0), (3, 1)]
    swap_y = [(e, e ^ 1) for e in range(8)]
    swap_x = [(d, d ^ 2) for d in range(4)]
    swap_core = [(d, d ^ 1) for d in range(4)]

    wide = width // 2
    pieces = [lax.reduce_precision(route_weight[0].T, 8, 7)]
    pieces.append(lax.reduce_precision(route_weight[0].T - pieces[0], 8, 7))
    pieces.append(route_weight[0].T - pieces[0] - pieces[1])
    own = call(
        pack_kernel,
        "pack",
        (),
        (),
        (cotangent, routing[0].T, jnp.concatenate(pieces, axis=0)),
        [pl.BlockSpec(memory_space=pltpu.VMEM)] * 3,
        (shape((tokens + 16, wide), jnp.bfloat16), shape((tokens, wide), jnp.bfloat16)),
        (pl.BlockSpec(memory_space=pltpu.VMEM),) * 2,
        moved=8 * tokens * width,
    )

    def permuted(parts, way):
        return [lax.ppermute(p, "expert", way) for p in parts]

    pair = permuted(own, swap_pair)
    middle_one = permuted(own, swap_middle)

    def tables(*given):
        spec = pl.BlockSpec((16, tokens), lambda i, m, e: (tokens // 16, 0))
        return call(
            table_kernel,
            "tables",
            (1,),
            (middle, experts),
            given,
            [spec] * len(given),
            (shape((2 * capacity, tokens), jnp.bfloat16), shape((2 * capacity, 1), jnp.float32)),
            (
                pl.BlockSpec((2 * capacity, tokens), lambda i, m, e: (0, 0)),
                pl.BlockSpec((2 * capacity, 1), lambda i, m, e: (0, 0)),
            ),
            moved=5 * capacity * tokens,
            flops=10 * capacity * tokens,
        )

    def pick(table, near, far, offset, columns, tile):
        halves, steps = len(near), columns // tile
        each, start = steps // halves, offset // tile
        specs = [
            pl.BlockSpec((2 * capacity, tokens), lambda i, m: (0, 0)),
            pl.BlockSpec((2 * capacity, 1), lambda i, m: (0, 0)),
        ]

        def place(h, i):
            return jnp.clip(i - h * each, 0, each - 1) if halves > 1 else i

        for h in range(halves):
            if far:
                specs.append(pl.BlockSpec((tokens, tile), lambda i, m, h=h: (0, (start + place(h, i)) * m[0])))
            else:
                specs.append(pl.BlockSpec((tokens, tile), lambda i, m, h=h: (0, start + place(h, i))))
        for h in range(len(far)):
            specs.append(pl.BlockSpec((tokens, tile), lambda i, m, h=h: (0, place(h, i) * (1 - m[0]))))
        out = shape((capacity, columns), jnp.bfloat16)
        mine, other = call(
            functools.partial(pick_kernel, halves, bool(far)),
            "pick",
            (steps,),
            (middle,),
            (*table, *near, *far),
            specs,
            (out, out),
            (pl.BlockSpec((capacity, tile), lambda i, m: (0, i)),) * 2,
            flops=4 * capacity * tokens * columns,
            moved=4 * (tokens + capacity) * columns,
        )
        return mine, other, lax.ppermute(other, "expert", swap_y)

    def back(place, pieces, previous):
        specs = [pl.BlockSpec(p.shape, lambda i, o: (0, 0)) for p in pieces]
        specs += [
            pl.BlockSpec((1, hidden_width, width), lambda i, o: (0, 0, 0)),
            pl.BlockSpec((1, 1, capacity, 2 * hidden_width), lambda i, o: (0, 0, o[place], 0)),
        ]
        ins = [*pieces, weight, saved_preact]
        aliases = {}
        if previous is not None:
            aliases = {len(ins): 0}
            ins.append(previous)
            specs.append(ANY)
        return call(
            functools.partial(back_kernel, len(pieces)),
            "back",
            (1,),
            (order,),
            ins,
            specs,
            shape(saved_preact.shape, jnp.bfloat16),
            pl.BlockSpec((1, 1, capacity, 2 * hidden_width), lambda i, o: (0, 0, o[place], 0)),
            aliases=aliases,
            flops=2 * capacity * hidden_width * width,
            moved=hidden_width * width + 6 * capacity * hidden_width + 2 * capacity * width,
        )

    mine0, other0, got0 = pick(tables(own[0]), own, (), 0, width, 512)
    turned = call(
        hidden_kernel,
        "hidden",
        (8,),
        (order, groups),
        (saved_preact,),
        [pl.BlockSpec((1, 1, capacity, 2 * hidden_width), lambda i, o, g: (0, 0, o[i], 0))],
        shape((hidden_width, slots), jnp.bfloat16),
        pl.BlockSpec((hidden_width, capacity), lambda i, o, g: (0, i)),
        scratch=[pltpu.VMEM((hidden_width, capacity), jnp.bfloat16)],
        moved=9 * slots * hidden_width,
        flops=40 * slots * hidden_width,
    )
    grad_preact = back(0, [mine0], None)
    middle_two = permuted(pair[:1], swap_middle)
    end_one = permuted(middle_one[:1], to_end)
    grad_preact = back(1, [got0], grad_preact)
    pair[1], middle_one[1], grad_preact, turned = after(pair[1], middle_one[1], grad_preact, turned)
    middle_two += permuted(pair[1:], swap_middle)
    end_one += permuted(middle_one[1:], to_end)
    mine1, other1, got1 = pick(tables(pair[0]), pair, (), 0, width, 512)
    grad_preact = back(2, [mine1], grad_preact)

    chunks = CHUNKS
    ends = []
    for offset, columns in chunks:
        half, inner = offset // wide, offset % wide
        count = tokens if offset else tokens + 16
        ends.append(lax.ppermute(middle_two[half][:count, inner : inner + columns], "expert", to_end))
    grad_preact = back(3, [got1], grad_preact)
    end_one[1], grad_preact = after(end_one[1], grad_preact)
    mine2, other2, got2 = pick(tables(middle_one[0], end_one[0]), middle_one, end_one, 0, width, 512)
    grad_preact = back(4, [mine2], grad_preact)
    ends[0], grad_preact = after(ends[0], grad_preact)
    last_table = tables(middle_two[0], ends[0])
    early = 6 * capacity

    def base_product(got2):
        return call(
            base_kernel,
            "base",
            (4,),
            (),
            (turned, mine0, got0, mine1, got1, mine2, got2),
            [pl.BlockSpec((hidden_width, early), lambda i: (0, 0))]
            + [pl.BlockSpec((capacity, width // 4), lambda i: (0, i))] * 6,
            shape((hidden_width, width), jnp.float32),
            pl.BlockSpec((hidden_width, width // 4), lambda i: (0, i)),
            flops=2 * hidden_width * early * width,
            moved=2 * (hidden_width * early + early * width) + 4 * hidden_width * width,
        )

    def last_block(chunk, end_two):
        offset, columns = chunk
        half, inner = offset // wide, offset % wide
        return pick(last_table, middle_two[half : half + 1], (end_two,), inner, columns, columns)

    def product(chunk, mine3, got3):
        offset, columns = chunk
        column = offset // columns
        half = shape((2 * rows, columns), jnp.bfloat16)
        part = pl.BlockSpec((capacity, columns), lambda i: (0, 0))
        return call(
            product_kernel,
            "product",
            (1,),
            (),
            (base, turned, mine3, got3),
            [
                pl.BlockSpec((hidden_width, columns), lambda i: (0, column)),
                pl.BlockSpec((hidden_width, 2 * capacity), lambda i: (0, 3)),
                part,
                part,
            ],
            (half, half),
            (pl.BlockSpec((2 * rows, columns), lambda i: (0, 0)),) * 2,
            flops=4 * hidden_width * capacity * columns,
            moved=4 * hidden_width * capacity + 6 * hidden_width * columns,
        )

    def adam(chunk, keep, near, far, previous):
        offset, columns = chunk
        column = offset // columns
        state = pl.BlockSpec((1, rows, columns), lambda i: (0, 0, column))
        second = pl.BlockSpec((rows, columns), lambda i: (1, 0))
        whole = pl.BlockSpec((rows, columns), lambda i: (0, 0))
        out_state = shape(master.shape, jnp.float32)
        return call(
            adam_kernel,
            "adam",
            (1,),
            (),
            (keep, near, far, master, moment1, moment2, *previous),
            [second, second, whole, state, state, state] + [ANY] * len(previous),
            (out_state, out_state, out_state, shape((rows, columns), jnp.bfloat16)),
            (state, state, state, whole),
            aliases={6 + k: k for k in range(len(previous))},
            flops=20 * rows * columns,
            moved=32 * rows * columns,
        )

    def assemble(chunk, fresh, crossed, sibling, last):
        offset, columns = chunk
        column = offset // columns
        return call(
            assemble_kernel,
            "assemble",
            (1,),
            (groups,),
            (fresh, crossed, sibling, *last),
            [
                pl.BlockSpec((rows, columns), lambda i, g: (0, 0)),
                pl.BlockSpec((rows, columns), lambda i, g: (0, 0)),
                pl.BlockSpec((2 * rows, columns), lambda i, g: (0, 0)),
            ]
            + [ANY] * len(last),
            shape((1, hidden_width, width), jnp.bfloat16),
            pl.BlockSpec((1, hidden_width, columns), lambda i, g: (0, 0, column)),
            aliases={3: 0} if last else None,
            moved=16 * rows * columns,
        )

    states, next_weight = (), ()
    total = len(chunks)
    mines, gots, others3 = [], [], []
    sends, keeps, nears, acrosses, fars = {}, {}, {}, {}, {}
    freshes, crosseds, siblings = {}, {}, {}

    def tied(value, token):
        return value if token is None else after(value, token)[0]

    def sum_core(k, token):
        sends[k], keeps[k] = product(chunks[k], mines[k], tied(gots[k], token))
        nears[k] = lax.ppermute(sends[k], "dp", swap_core)
        return sends[k]

    def sum_x(k, token):
        near = tied(nears[k], token)
        acrosses[k] = (keeps[k][:rows].astype(jnp.float32) + near[:rows].astype(jnp.float32)).astype(jnp.bfloat16)
        nears[k] = near
        fars[k] = lax.ppermute(acrosses[k], "dp", swap_x)
        return acrosses[k]

    def update(k, token):
        nonlocal states
        *states, freshes[k] = adam(chunks[k], keeps[k], nears[k], tied(fars[k], token), states)
        crosseds[k] = lax.ppermute(freshes[k], "dp", swap_x)
        return freshes[k]

    def gather_core(k, token):
        crosseds[k] = tied(crosseds[k], token)
        both = jnp.concatenate([freshes[k], crosseds[k]], axis=0)
        siblings[k] = lax.ppermute(both, "dp", swap_core)
        return both

    def gathered(k, token):
        nonlocal next_weight
        next_weight = (assemble(chunks[k], freshes[k], crosseds[k], tied(siblings[k], token), next_weight),)
        return next_weight[0]

    stages = (sum_core, sum_x, update, gather_core, gathered)
    for k in range(total):
        mine3, other3, got3 = last_block(chunks[k], ends[k])
        mines.append(mine3)
        gots.append(got3)
        done = []
        if k == 0:
            got2, _ = after(got2, other3)
            grad_preact = back(5, [got2], grad_preact)
            done = [grad_preact, base_product(got2)]
            base = done[1]
        for lag, stage in enumerate(stages):
            if k - 1 - lag >= 0:
                done.append(stage(k - 1 - lag, other3))
        if k + 1 < total:
            ends[k + 1], *done = after(ends[k + 1], *done)
            if k == 0:
                grad_preact, base = done
    grad_preact = back(6, mines, grad_preact)
    for k in range(total, total + len(stages)):
        for lag, stage in reversed(tuple(enumerate(stages))):
            if 0 <= k - 1 - lag < total:
                stage(k - 1 - lag, None)
    gots[-1], _ = after(gots[-1], acrosses[total - 1])
    grad_preact = back(7, gots, grad_preact)
    return (grad_preact, next_weight[0], *states)


def body(cotangent, routing, route_weight, saved_preact, weight, master, moment1, moment2):
    n_expert = lax.axis_size("expert")
    tokens = cotangent[0]
    width = tokens.shape[1]
    slots = saved_preact.shape[2]
    hidden_width = weight.shape[1]
    capacity = slots // n_expert
    route_count = routing.shape[2]
    chosen = routing[0].reshape(-1)
    onehot = (chosen[:, None] == jnp.arange(n_expert, dtype=jnp.int32)[None, :]).astype(jnp.int32)
    earlier = jnp.cumsum(onehot, axis=0) - onehot
    position = jnp.sum(earlier * onehot, axis=1)
    target = chosen * capacity + position
    source_token = jnp.arange(chosen.shape[0], dtype=jnp.int32) // route_count
    token_table = jnp.zeros((slots,), jnp.int32).at[target].set(source_token)
    weight_table = jnp.zeros((slots,), jnp.float32).at[target].set(route_weight[0].reshape(-1))
    scaled = (tokens[token_table].astype(jnp.float32) * weight_table[:, None]).astype(jnp.bfloat16)
    arrived = lax.all_to_all(
        scaled.reshape(n_expert, capacity, width), "expert", split_axis=0, concat_axis=0, tiled=True
    )
    arrived = arrived.reshape(slots, width)
    preact = saved_preact[0, 0].astype(jnp.float32)
    gate_value = preact[:, :hidden_width]
    up_value = preact[:, hidden_width:]
    sigmoid_gate = jax.nn.sigmoid(gate_value)
    activated = gate_value * sigmoid_gate
    hidden = (activated * up_value).astype(jnp.bfloat16)
    back = lax.dot_general(
        arrived, weight[0], (((1,), (1,)), ((), ())), preferred_element_type=jnp.float32
    )
    grad_gate = back * up_value * sigmoid_gate * (1.0 + gate_value * (1.0 - sigmoid_gate))
    grad_up = back * activated
    grad_preact = jnp.concatenate([grad_gate, grad_up], axis=1).astype(jnp.bfloat16)[None, None]
    gradient = lax.psum_scatter(
        lax.dot_general(
            hidden, arrived, (((0,), (0,)), ((), ())), preferred_element_type=jnp.float32
        ).astype(jnp.bfloat16),
        "dp",
        scatter_dimension=0,
        tiled=True,
    ).astype(jnp.float32)
    moment_one = beta_first * moment1[0] + (1.0 - beta_first) * gradient
    moment_two = beta_second * moment2[0] + (1.0 - beta_second) * gradient * gradient
    step_size = (
        moment_one / bias_first / (jnp.sqrt(moment_two / bias_second) + adam_epsilon)
        + decay_rate * master[0]
    )
    master_next = master[0] - learn_rate * step_size
    weight_next = lax.all_gather(master_next.astype(jnp.bfloat16), "dp", axis=0, tiled=True)
    return (grad_preact, weight_next[None], master_next[None], moment_one[None], moment_two[None])


def solution(mesh):
    placed = (
        P("dp", "expert", None),
        P("dp", "expert", None),
        P("dp", "expert", None),
        P("dp", "expert", None, None),
        P("expert", None, None),
        P("expert", "dp", None),
        P("expert", "dp", None),
        P("expert", "dp", None),
    )
    line = mesh.shape["expert"] == 8 and mesh.shape["dp"] == 4
    return jax.shard_map(
        line_body if line else body,
        mesh=mesh,
        in_specs=placed,
        out_specs=(
            P("dp", "expert", None, None),
            P("expert", None, None),
            P("expert", "dp", None),
            P("expert", "dp", None),
            P("expert", "dp", None),
        ),
        check_vma=False,
    )
```

```python
import functools

import jax
import jax.numpy as jnp
from jax import lax
from jax.experimental import pallas as pl
from jax.experimental.pallas import tpu as pltpu
from jax.sharding import PartitionSpec as P

beta_first = 0.9
beta_second = 0.95
bias_first = 1.0 - 0.9**10
bias_second = 1.0 - 0.95**10
adam_epsilon = 1e-08
learn_rate = 0.001
decay_rate = 0.1

VMEM_LIMIT = 24 * 1024 * 1024
COST = 4096
EARLY = False
CLAIM = 3_000_000_000
TILE = 256
HALF = 1280
PACK_LIMIT = 56 * 1024 * 1024
SENT = ((0, 512), (512, 768), (1280, 768))
CHUNKS = ((0, 512), (512, 768), (1280, 512), (1792, 256))
ANY = pl.BlockSpec(memory_space=pl.ANY)


def params(limit):
    return pltpu.CompilerParams(vmem_limit_bytes=limit)


def call(kernel, name, grid, scalars, ins, specs, outs, out_specs, scratch=(), aliases=None, flops=0, moved=0, limit=VMEM_LIMIT):
    shift = len(scalars)
    return pl.pallas_call(
        kernel,
        name=name,
        grid_spec=pltpu.PrefetchScalarGridSpec(
            num_scalar_prefetch=shift,
            grid=grid,
            in_specs=specs,
            out_specs=out_specs,
            scratch_shapes=list(scratch),
        ),
        out_shape=outs,
        input_output_aliases={shift + a: b for a, b in (aliases or {}).items()},
        compiler_params=params(limit),
        cost_estimate=pl.CostEstimate(flops=flops // COST, bytes_accessed=moved // COST, transcendentals=0),
    )(*scalars, *ins)


def after(*values):
    return lax.optimization_barrier(values)


def shape(dims, dtype):
    return jax.ShapeDtypeStruct(dims, dtype)


def hidden_kernel(order, groups, preact, out, turned):
    width = preact.shape[-1] // 2
    gate = preact[0, 0, :, :width].astype(jnp.float32)
    up = preact[0, 0, :, width:].astype(jnp.float32)
    value = gate * jax.nn.sigmoid(gate) * up
    turned[...] = value.T.astype(jnp.bfloat16)
    rows = width // 4
    for g in range(4):
        start = pl.multiple_of(groups[g] * rows, 16)
        out[g * rows : (g + 1) * rows, :] = turned[pl.ds(start, rows), :]


def pack_kernel(tokens, chosen, weights, packed):
    last = pl.program_id(0) == pl.num_programs(0) - 1

    @pl.when(jnp.logical_not(last))
    def _():
        packed[...] = tokens[0]

    @pl.when(last)
    def _():
        length = chosen.shape[1]
        packed[...] = jnp.zeros_like(packed)
        packed[:8, :length] = jnp.concatenate([chosen[...].astype(jnp.float32), weights[...]], axis=0).astype(
            jnp.bfloat16
        )


def table_kernel(middle, experts, *refs):
    infos, picks, scales = refs[:-2], refs[-2], refs[-1]
    info = infos[0][...].astype(jnp.float32)
    if len(infos) == 2:
        info = jnp.where(middle[0] == 1, info, infos[1][...].astype(jnp.float32))
    capacity = picks.shape[0] // 2
    tokens = info.shape[1]
    first, second = info[0:1, :], info[1:2, :]
    weight_one = (info[2:3, :] + info[4:5, :]) + info[6:7, :]
    weight_two = (info[3:4, :] + info[5:6, :]) + info[7:8, :]
    before = lax.broadcasted_iota(jnp.int32, (tokens, tokens), 0)
    after = lax.broadcasted_iota(jnp.int32, (tokens, tokens), 1)
    earlier = (before < after).astype(jnp.float32).astype(jnp.bfloat16)
    for k in range(2):
        expert = experts[k].astype(jnp.float32)
        is_first = first == expert
        named = jnp.logical_or(is_first, second == expert)
        flag = jnp.where(named, 1.0, 0.0)
        position = jnp.dot(
            jnp.broadcast_to(flag, (16, tokens)).astype(jnp.bfloat16), earlier, preferred_element_type=jnp.float32
        )[0:1, :]
        place = jnp.where(named, position, -1.0).astype(jnp.int32)
        slot = lax.broadcasted_iota(jnp.int32, (capacity, tokens), 0)
        hit = slot == place
        value = jnp.where(is_first, weight_one, weight_two)
        picks[k * capacity : (k + 1) * capacity, :] = jnp.where(hit, 1.0, 0.0).astype(jnp.bfloat16)
        scales[k * capacity : (k + 1) * capacity, :] = jnp.sum(jnp.where(hit, value, 0.0), axis=1, keepdims=True)


def pick_kernel(firsts, both, middle, picks, scales, *refs):
    halves = len(firsts)
    near, far, (mine, other) = refs[:halves], refs[halves:-2], refs[-2:]
    capacity = mine.shape[0]

    def step(k):
        rows = jnp.where(middle[0] == 1, near[k][...], far[k][...]) if both else near[k][...]
        value = jnp.dot(picks[...], rows, preferred_element_type=jnp.float32) * scales[...]
        mine[...] = value[:capacity].astype(jnp.bfloat16)
        other[...] = value[capacity:].astype(jnp.bfloat16)

    if halves == 1:
        step(0)
    else:
        late = pl.program_id(0) >= firsts[1]
        pl.when(jnp.logical_not(late))(functools.partial(step, 0))
        pl.when(late)(functools.partial(step, 1))


def base_kernel(turned, *refs):
    pieces, out = refs[:-1], refs[-1]
    rows = jnp.concatenate([p[...] for p in pieces], axis=0)
    out[...] = jnp.dot(turned[...], rows, preferred_element_type=jnp.float32)


def product_kernel(base, turned, mine, got, send, keep):
    half = send.shape[0]
    rows = jnp.concatenate([mine[...], got[...]], axis=0)
    total = base[...] + jnp.dot(turned[...], rows, preferred_element_type=jnp.float32)
    send[...] = total[:half].astype(jnp.bfloat16)
    keep[...] = total[half:].astype(jnp.bfloat16)


def back_kernel(count, order, *refs):
    pieces = refs[:count]
    weight, preact, out = refs[count], refs[count + 1], refs[-1]
    width = weight.shape[1]
    rows = jnp.concatenate([p[...] for p in pieces], axis=1)
    back = lax.dot_general(rows, weight[0], (((1,), (1,)), ((), ())), preferred_element_type=jnp.float32)
    gate = preact[0, 0, :, :width].astype(jnp.float32)
    up = preact[0, 0, :, width:].astype(jnp.float32)
    sig = jax.nn.sigmoid(gate)
    out[0, 0, :, :width] = (back * up * sig * (1.0 + gate * (1.0 - sig))).astype(jnp.bfloat16)
    out[0, 0, :, width:] = (back * (gate * sig)).astype(jnp.bfloat16)


def adam_kernel(kept, near, far, master, moment1, moment2, *refs):
    out_master, out_one, out_two, out_weight = refs[-4:]
    gradient = (kept[...].astype(jnp.float32) + near[...].astype(jnp.float32)) + far[...].astype(jnp.float32)
    moment_one = beta_first * moment1[0] + (1.0 - beta_first) * gradient
    moment_two = beta_second * moment2[0] + (1.0 - beta_second) * gradient * gradient
    step_size = (
        moment_one / bias_first / (jnp.sqrt(moment_two / bias_second) + adam_epsilon) + decay_rate * master[0]
    )
    master_next = master[0] - learn_rate * step_size
    out_master[0] = master_next
    out_one[0] = moment_one
    out_two[0] = moment_two
    out_weight[...] = master_next.astype(jnp.bfloat16)


def assemble_kernel(places, own, across, sibling, *refs):
    out = refs[-1]
    rows = own.shape[0]

    def put(g, value):
        out[0, pl.ds(pl.multiple_of(places[g] * rows, 16), rows), :] = value

    put(3, own[...])
    put(2, across[...])
    put(1, sibling[:rows, :])
    put(0, sibling[rows:, :])


def line_body(cotangent, routing, route_weight, saved_preact, weight, master, moment1, moment2):
    tokens, width = cotangent.shape[1:]
    slots, hidden_width = saved_preact.shape[2], weight.shape[1]
    capacity = slots // 8
    rows = hidden_width // 4
    expert = lax.axis_index("expert")
    replica = lax.axis_index("dp")
    z, y = expert // 2, expert % 2
    x, core = replica // 2, replica % 2
    middle = jnp.where((z == 1) | (z == 2), 1, 0).astype(jnp.int32).reshape(1)
    lower = z < 2
    blocks = [z, z ^ 1, jnp.where(lower, 2, 1), jnp.where(lower, 3, 0)]
    order = jnp.stack([b * 2 + s for b in blocks for s in (y, 1 - y)]).astype(jnp.int32)
    experts = jnp.stack([expert, expert ^ 1]).astype(jnp.int32)
    groups = jnp.stack([(1 - x) * 2 + 1 - core, x * 2 + 1 - core, (1 - x) * 2 + core, x * 2 + core]).astype(jnp.int32)

    swap_pair = [(e, e ^ 2) for e in range(8)]
    swap_middle = [(2, 4), (4, 2), (3, 5), (5, 3)]
    to_end = [(4, 6), (5, 7), (2, 0), (3, 1)]
    swap_y = [(e, e ^ 1) for e in range(8)]
    swap_x = [(d, d ^ 2) for d in range(4)]
    swap_core = [(d, d ^ 1) for d in range(4)]

    wide = HALF
    pieces = [lax.reduce_precision(route_weight[0].T, 8, 7)]
    pieces.append(lax.reduce_precision(route_weight[0].T - pieces[0], 8, 7))
    pieces.append(route_weight[0].T - pieces[0] - pieces[1])
    step = 128
    count = tokens // step
    packed = call(
        pack_kernel,
        "pack",
        (count + 1,),
        (),
        (cotangent, routing[0].T, jnp.concatenate(pieces, axis=0)),
        [
            pl.BlockSpec((1, step, wide), lambda i: (0, jnp.minimum(i, count - 1), 0)),
            pl.BlockSpec((2, tokens), lambda i: (0, 0)),
            pl.BlockSpec((6, tokens), lambda i: (0, 0)),
        ],
        shape((tokens + 16, wide), jnp.bfloat16),
        pl.BlockSpec((step, wide), lambda i: (i, 0)),
        moved=4 * tokens * width,
        limit=PACK_LIMIT,
    )
    own = [packed, cotangent[0, :, wide:]]

    def permuted(parts, way):
        return [lax.ppermute(p, "expert", way) for p in parts]

    pair = permuted(own, swap_pair)
    middle_one = permuted(own, swap_middle)

    def tables(*given):
        spec = pl.BlockSpec((16, tokens), lambda i, m, e: (tokens // 16, 0))
        return call(
            table_kernel,
            "tables",
            (1,),
            (middle, experts),
            given,
            [spec] * len(given),
            (shape((2 * capacity, tokens), jnp.bfloat16), shape((2 * capacity, 1), jnp.float32)),
            (
                pl.BlockSpec((2 * capacity, tokens), lambda i, m, e: (0, 0)),
                pl.BlockSpec((2 * capacity, 1), lambda i, m, e: (0, 0)),
            ),
            moved=5 * capacity * tokens,
            flops=10 * capacity * tokens,
        )

    def pick(table, near, far, offset, columns, tile=TILE, claim=0, late=0):
        steps, start = columns // tile, offset // tile
        counts = [p.shape[1] // tile for p in near] if len(near) > 1 else [steps]
        firsts = [sum(counts[:h]) for h in range(len(counts))]
        specs = [
            pl.BlockSpec((2 * capacity, tokens), lambda i, m: (0, 0)),
            pl.BlockSpec((2 * capacity, 1), lambda i, m: (0, 0)),
        ]

        def place(h, i):
            return jnp.clip(i - firsts[h], 0, counts[h] - 1) if len(counts) > 1 else i

        for h in range(len(near)):
            if far:
                specs.append(pl.BlockSpec((tokens, tile), lambda i, m, h=h: (0, (start + place(h, i)) * m[0])))
            else:
                specs.append(pl.BlockSpec((tokens, tile), lambda i, m, h=h: (0, start + place(h, i))))
        for h in range(len(far)):
            specs.append(pl.BlockSpec((tokens, tile), lambda i, m, h=h: (0, (late // tile + place(h, i)) * (1 - m[0]))))
        out = shape((capacity, columns), jnp.bfloat16)
        mine, other = call(
            functools.partial(pick_kernel, firsts, bool(far)),
            "pick",
            (steps,),
            (middle,),
            (*table, *near, *far),
            specs,
            (out, out),
            (pl.BlockSpec((capacity, tile), lambda i, m: (0, i)),) * 2,
            flops=4 * capacity * tokens * columns + claim * COST,
            moved=4 * (tokens + capacity) * columns,
        )
        return mine, other, lax.ppermute(other, "expert", swap_y)

    def back(place, pieces, previous):
        specs = [pl.BlockSpec(p.shape, lambda i, o: (0, 0)) for p in pieces]
        specs += [
            pl.BlockSpec((1, hidden_width, width), lambda i, o: (0, 0, 0)),
            pl.BlockSpec((1, 1, capacity, 2 * hidden_width), lambda i, o: (0, 0, o[place], 0)),
        ]
        ins = [*pieces, weight, saved_preact]
        aliases = {}
        if previous is not None:
            aliases = {len(ins): 0}
            ins.append(previous)
            specs.append(ANY)
        return call(
            functools.partial(back_kernel, len(pieces)),
            "back",
            (1,),
            (order,),
            ins,
            specs,
            shape(saved_preact.shape, jnp.bfloat16),
            pl.BlockSpec((1, 1, capacity, 2 * hidden_width), lambda i, o: (0, 0, o[place], 0)),
            aliases=aliases,
            flops=2 * capacity * hidden_width * width,
            moved=hidden_width * width + 6 * capacity * hidden_width + 2 * capacity * width,
        )

    mine0, other0, got0 = pick(tables(own[0]), own, (), 0, width)
    turned = call(
        hidden_kernel,
        "hidden",
        (8,),
        (order, groups),
        (saved_preact,),
        [pl.BlockSpec((1, 1, capacity, 2 * hidden_width), lambda i, o, g: (0, 0, o[i], 0))],
        shape((hidden_width, slots), jnp.bfloat16),
        pl.BlockSpec((hidden_width, capacity), lambda i, o, g: (0, i)),
        scratch=[pltpu.VMEM((hidden_width, capacity), jnp.bfloat16)],
        moved=9 * slots * hidden_width,
        flops=40 * slots * hidden_width,
    )
    grad_preact = back(0, [mine0], None)
    pair[0], middle_one[0], grad_preact, turned = after(pair[0], middle_one[0], grad_preact, turned)
    middle_two = permuted(pair[:1], swap_middle)
    end_one = permuted(middle_one[:1], to_end)
    grad_preact = back(1, [got0], grad_preact)
    pair[1], middle_one[1], grad_preact = after(pair[1], middle_one[1], grad_preact)
    middle_two += permuted(pair[1:], swap_middle)
    end_one += permuted(middle_one[1:], to_end)
    mine1, other1, got1 = pick(tables(pair[0]), pair, (), 0, width)
    grad_preact = back(2, [mine1], grad_preact)
    middle_two[0], end_one[0], grad_preact, got1 = after(middle_two[0], end_one[0], grad_preact, got1)

    chunks = CHUNKS

    early = 6 * capacity

    def base_product(half, mine2, got2):
        columns = mine2.shape[1]
        start = half * wide // TILE
        full = pl.BlockSpec((capacity, TILE), lambda i: (0, start + i))
        part = pl.BlockSpec((capacity, TILE), lambda i: (0, i))
        return call(
            base_kernel,
            "base",
            (columns // TILE,),
            (),
            (turned, mine0, got0, mine1, got1, mine2, got2),
            [pl.BlockSpec((hidden_width, early), lambda i: (0, 0))] + [full] * 4 + [part] * 2,
            shape((hidden_width, columns), jnp.float32),
            pl.BlockSpec((hidden_width, TILE), lambda i: (0, i)),
            flops=2 * hidden_width * early * columns,
            moved=2 * (hidden_width * early + early * columns) + 4 * hidden_width * columns,
        )

    def to_ends(half):
        sent = []
        for offset, columns in SENT:
            if (offset >= wide) == half:
                inner = offset - wide * half
                count = tokens if offset else tokens + 16
                sent.append(lax.ppermute(middle_two[half][:count, inner : inner + columns], "expert", to_end))
        return sent

    ends = to_ends(0)
    table2 = tables(middle_one[0], end_one[0])
    mine2, other2, got2 = pick(table2, middle_one[:1], end_one[:1], 0, wide, wide // 2)
    mine2, got2 = [mine2], [got2]
    grad_preact = back(3, [got1], grad_preact)
    middle_two[1], end_one[1], grad_preact, other2 = after(middle_two[1], end_one[1], grad_preact, other2)
    ends += to_ends(1)
    mine2b, other2, got2b = pick(table2, middle_one[1:], end_one[1:], 0, width - wide, width - wide)
    mine2.append(mine2b)
    got2.append(got2b)
    grad_preact = back(4, mine2, grad_preact)
    bases = [base_product(0, mine2[0], got2[0])]
    ends[0], grad_preact, bases[0] = after(ends[0], grad_preact, bases[0])
    last_table = tables(middle_two[0], ends[0])

    def last_block(k, chunk, end_two):
        offset, columns = chunk
        half = offset >= wide
        inner = offset - wide * half
        late = offset - SENT[k][0]
        return pick(last_table, (middle_two[half],), (end_two,), inner, columns, claim=CLAIM, late=late)

    def product(chunk, mine3, got3):
        offset, columns = chunk
        side = int(offset >= wide)
        start = (offset - wide * side) // TILE
        half = shape((2 * rows, columns), jnp.bfloat16)
        part = pl.BlockSpec((capacity, TILE), lambda i: (0, i))
        return call(
            product_kernel,
            "product",
            (columns // TILE,),
            (),
            (bases[side], turned, mine3, got3),
            [
                pl.BlockSpec((hidden_width, TILE), lambda i: (0, start + i)),
                pl.BlockSpec((hidden_width, 2 * capacity), lambda i: (0, 3)),
                part,
                part,
            ],
            (half, half),
            (pl.BlockSpec((2 * rows, TILE), lambda i: (0, i)),) * 2,
            flops=4 * hidden_width * capacity * columns,
            moved=4 * hidden_width * capacity + 6 * hidden_width * columns,
        )

    def adam(chunk, keep, near, far, previous):
        offset, columns = chunk
        start = offset // TILE
        state = pl.BlockSpec((1, rows, TILE), lambda i: (0, 0, start + i))
        second = pl.BlockSpec((rows, TILE), lambda i: (1, i))
        whole = pl.BlockSpec((rows, TILE), lambda i: (0, i))
        out_state = shape(master.shape, jnp.float32)
        return call(
            adam_kernel,
            "adam",
            (columns // TILE,),
            (),
            (keep, near, far, master, moment1, moment2, *previous),
            [second, second, whole, state, state, state] + [ANY] * len(previous),
            (out_state, out_state, out_state, shape((rows, columns), jnp.bfloat16)),
            (state, state, state, whole),
            aliases={6 + k: k for k in range(len(previous))},
            flops=20 * rows * columns,
            moved=32 * rows * columns,
        )

    def assemble(chunk, fresh, crossed, sibling, last):
        offset, columns = chunk
        start = offset // TILE
        return call(
            assemble_kernel,
            "assemble",
            (columns // TILE,),
            (groups,),
            (fresh, crossed, sibling, *last),
            [
                pl.BlockSpec((rows, TILE), lambda i, g: (0, i)),
                pl.BlockSpec((rows, TILE), lambda i, g: (0, i)),
                pl.BlockSpec((2 * rows, TILE), lambda i, g: (0, i)),
            ]
            + [ANY] * len(last),
            shape((1, hidden_width, width), jnp.bfloat16),
            pl.BlockSpec((1, hidden_width, TILE), lambda i, g: (0, 0, start + i)),
            aliases={3: 0} if last else None,
            moved=16 * rows * columns,
        )

    states, next_weight = (), ()
    mines, gots, others3 = [], [], []
    sends, keeps, nears, acrosses, fars = {}, {}, {}, {}, {}
    freshes, crosseds, siblings = {}, {}, {}

    def tied(value, token):
        return value if token is None else after(value, token)[0]

    def sum_core(k, token):
        sends[k], keeps[k] = product(chunks[k], mines[k], tied(gots[k], token))
        nears[k] = lax.ppermute(sends[k], "dp", swap_core)
        return sends[k]

    def sum_x(k, token):
        near = tied(nears[k], token)
        acrosses[k] = (keeps[k][:rows].astype(jnp.float32) + near[:rows].astype(jnp.float32)).astype(jnp.bfloat16)
        nears[k] = near
        fars[k] = lax.ppermute(acrosses[k], "dp", swap_x)
        return acrosses[k]

    def update(k, token):
        nonlocal states
        *states, freshes[k] = adam(chunks[k], keeps[k], nears[k], tied(fars[k], token), states)
        crosseds[k] = lax.ppermute(freshes[k], "dp", swap_x)
        return freshes[k]

    def gather_core(k, token):
        crosseds[k] = tied(crosseds[k], token)
        both = jnp.concatenate([freshes[k], crosseds[k]], axis=0)
        siblings[k] = lax.ppermute(both, "dp", swap_core)
        return both

    def gathered(k, token):
        nonlocal next_weight
        next_weight = (assemble(chunks[k], freshes[k], crosseds[k], tied(siblings[k], token), next_weight),)
        return next_weight[0]

    def arrive(k, chunk):
        mine3, other3, got3 = last_block(k, chunks[chunk], ends[k])
        mines.append(mine3)
        gots.append(got3)
        return other3

    other = arrive(0, 0)
    got2[1], _ = after(got2[1], other)
    bases.append(base_product(1, mine2[1], got2[1]))
    sum_core(0, bases[1])
    if EARLY:
        across = sum_x(0, None)
        ends[1], across = after(ends[1], across)
    else:
        ends[1], send = after(ends[1], sends[0])
    other = arrive(1, 1)
    if not EARLY:
        other = sum_x(0, other)
    fresh = update(0, other)
    got2[1], fresh = after(got2[1], fresh)
    grad_preact = back(5, got2, grad_preact)
    sum_core(1, grad_preact)
    ends[2], send = after(ends[2], sends[1])
    across = sum_x(1, ends[2])
    ends[2], across = after(ends[2], across)
    arrive(2, 2)
    other = arrive(2, 3)
    both = gather_core(0, other)
    fresh = update(1, both)
    send = sum_core(2, fresh)
    send = sum_core(3, send)
    across = sum_x(2, send)
    across = sum_x(3, across)
    mines[0], _ = after(mines[0], across)
    grad_preact = back(6, mines, grad_preact)
    placed = gathered(0, grad_preact)
    fresh = update(2, placed)
    fresh = update(3, fresh)
    both = gather_core(1, fresh)
    gots[0], _ = after(gots[0], both)
    grad_preact = back(7, gots, grad_preact)
    placed = gathered(1, grad_preact)
    both = gather_core(2, placed)
    gather_core(3, both)
    gathered(2, None)
    gathered(3, None)
    return (grad_preact, next_weight[0], *states)


def body(cotangent, routing, route_weight, saved_preact, weight, master, moment1, moment2):
    n_expert = lax.axis_size("expert")
    tokens = cotangent[0]
    width = tokens.shape[1]
    slots = saved_preact.shape[2]
    hidden_width = weight.shape[1]
    capacity = slots // n_expert
    route_count = routing.shape[2]
    chosen = routing[0].reshape(-1)
    onehot = (chosen[:, None] == jnp.arange(n_expert, dtype=jnp.int32)[None, :]).astype(jnp.int32)
    earlier = jnp.cumsum(onehot, axis=0) - onehot
    position = jnp.sum(earlier * onehot, axis=1)
    target = chosen * capacity + position
    source_token = jnp.arange(chosen.shape[0], dtype=jnp.int32) // route_count
    token_table = jnp.zeros((slots,), jnp.int32).at[target].set(source_token)
    weight_table = jnp.zeros((slots,), jnp.float32).at[target].set(route_weight[0].reshape(-1))
    scaled = (tokens[token_table].astype(jnp.float32) * weight_table[:, None]).astype(jnp.bfloat16)
    arrived = lax.all_to_all(
        scaled.reshape(n_expert, capacity, width), "expert", split_axis=0, concat_axis=0, tiled=True
    )
    arrived = arrived.reshape(slots, width)
    preact = saved_preact[0, 0].astype(jnp.float32)
    gate_value = preact[:, :hidden_width]
    up_value = preact[:, hidden_width:]
    sigmoid_gate = jax.nn.sigmoid(gate_value)
    activated = gate_value * sigmoid_gate
    hidden = (activated * up_value).astype(jnp.bfloat16)
    back = lax.dot_general(
        arrived, weight[0], (((1,), (1,)), ((), ())), preferred_element_type=jnp.float32
    )
    grad_gate = back * up_value * sigmoid_gate * (1.0 + gate_value * (1.0 - sigmoid_gate))
    grad_up = back * activated
    grad_preact = jnp.concatenate([grad_gate, grad_up], axis=1).astype(jnp.bfloat16)[None, None]
    gradient = lax.psum_scatter(
        lax.dot_general(
            hidden, arrived, (((0,), (0,)), ((), ())), preferred_element_type=jnp.float32
        ).astype(jnp.bfloat16),
        "dp",
        scatter_dimension=0,
        tiled=True,
    ).astype(jnp.float32)
    moment_one = beta_first * moment1[0] + (1.0 - beta_first) * gradient
    moment_two = beta_second * moment2[0] + (1.0 - beta_second) * gradient * gradient
    step_size = (
        moment_one / bias_first / (jnp.sqrt(moment_two / bias_second) + adam_epsilon)
        + decay_rate * master[0]
    )
    master_next = master[0] - learn_rate * step_size
    weight_next = lax.all_gather(master_next.astype(jnp.bfloat16), "dp", axis=0, tiled=True)
    return (grad_preact, weight_next[None], master_next[None], moment_one[None], moment_two[None])


def solution(mesh):
    placed = (
        P("dp", "expert", None),
        P("dp", "expert", None),
        P("dp", "expert", None),
        P("dp", "expert", None, None),
        P("expert", None, None),
        P("expert", "dp", None),
        P("expert", "dp", None),
        P("expert", "dp", None),
    )
    line = mesh.shape["expert"] == 8 and mesh.shape["dp"] == 4
    return jax.shard_map(
        line_body if line else body,
        mesh=mesh,
        in_specs=placed,
        out_specs=(
            P("dp", "expert", None, None),
            P("expert", None, None),
            P("expert", "dp", None),
            P("expert", "dp", None),
            P("expert", "dp", None),
        ),
        check_vma=False,
    )
```

```python
import functools

import jax
import jax.numpy as jnp
from jax import lax
from jax.experimental import pallas as pl
from jax.experimental.pallas import tpu as pltpu
from jax.sharding import PartitionSpec as P

beta_first = 0.9
beta_second = 0.95
bias_first = 1.0 - 0.9**10
bias_second = 1.0 - 0.95**10
adam_epsilon = 1e-08
learn_rate = 0.001
decay_rate = 0.1

VMEM_LIMIT = 24 * 1024 * 1024
COST = 4096
EARLY = False
CLAIM = 3_000_000_000
TILE = 256
HALF = 1280
PACK_LIMIT = 56 * 1024 * 1024
SENT = ((0, 512), (512, 768), (1280, 768))
CHUNKS = ((0, 512), (512, 768), (1280, 512), (1792, 256))
ANY = pl.BlockSpec(memory_space=pl.ANY)


def params(limit):
    return pltpu.CompilerParams(vmem_limit_bytes=limit)


def call(kernel, name, grid, scalars, ins, specs, outs, out_specs, scratch=(), aliases=None, flops=0, moved=0, limit=VMEM_LIMIT):
    shift = len(scalars)
    return pl.pallas_call(
        kernel,
        name=name,
        grid_spec=pltpu.PrefetchScalarGridSpec(
            num_scalar_prefetch=shift,
            grid=grid,
            in_specs=specs,
            out_specs=out_specs,
            scratch_shapes=list(scratch),
        ),
        out_shape=outs,
        input_output_aliases={shift + a: b for a, b in (aliases or {}).items()},
        compiler_params=params(limit),
        cost_estimate=pl.CostEstimate(flops=flops // COST, bytes_accessed=moved // COST, transcendentals=0),
    )(*scalars, *ins)


def after(*values):
    return lax.optimization_barrier(values)


def shape(dims, dtype):
    return jax.ShapeDtypeStruct(dims, dtype)


def hidden_kernel(order, groups, preact, out, turned):
    width = preact.shape[-1] // 2
    gate = preact[0, 0, :, :width].astype(jnp.float32)
    up = preact[0, 0, :, width:].astype(jnp.float32)
    value = gate * jax.nn.sigmoid(gate) * up
    turned[...] = value.T.astype(jnp.bfloat16)
    rows = width // 4
    for g in range(4):
        start = pl.multiple_of(groups[g] * rows, 16)
        out[g * rows : (g + 1) * rows, :] = turned[pl.ds(start, rows), :]


def pack_kernel(tokens, chosen, weights, packed, held, into, out):
    count, wide = tokens.shape[1], packed.shape[1]
    parts = 8
    part = count // parts
    loads, stores = [], []
    for k in range(parts):
        here = pl.ds(k * part, part)
        loads.append(pltpu.make_async_copy(tokens.at[0, here, pl.ds(0, wide)], held.at[here, :], into.at[k]))
        stores.append(pltpu.make_async_copy(held.at[here, :], packed.at[here, :], out.at[k]))
    tail = pl.ds(count, 16)
    stores.append(pltpu.make_async_copy(held.at[tail, :], packed.at[tail, :], out.at[parts]))
    for load in loads:
        load.start()
    exact = weights[...]
    high = exact.astype(jnp.bfloat16).astype(jnp.float32)
    middle = (exact - high).astype(jnp.bfloat16).astype(jnp.float32)
    low = exact - high - middle
    info = jnp.concatenate([chosen[...].astype(jnp.float32), high, middle, low, jnp.zeros((8, count))], axis=0)
    held[count:, :] = jnp.zeros((16, wide), jnp.bfloat16)
    held[count:, :count] = info.astype(jnp.bfloat16)
    stores[parts].start()
    for k in range(parts):
        loads[k].wait()
        stores[k].start()
    for store in stores:
        store.wait()


def table_kernel(middle, experts, *refs):
    infos, picks, scales = refs[:-2], refs[-2], refs[-1]
    info = infos[0][...].astype(jnp.float32)
    if len(infos) == 2:
        info = jnp.where(middle[0] == 1, info, infos[1][...].astype(jnp.float32))
    capacity = picks.shape[0] // 2
    tokens = info.shape[1]
    first, second = info[0:1, :], info[1:2, :]
    weight_one = (info[2:3, :] + info[4:5, :]) + info[6:7, :]
    weight_two = (info[3:4, :] + info[5:6, :]) + info[7:8, :]
    before = lax.broadcasted_iota(jnp.int32, (tokens, tokens), 0)
    after = lax.broadcasted_iota(jnp.int32, (tokens, tokens), 1)
    earlier = (before < after).astype(jnp.float32).astype(jnp.bfloat16)
    for k in range(2):
        expert = experts[k].astype(jnp.float32)
        is_first = first == expert
        named = jnp.logical_or(is_first, second == expert)
        flag = jnp.where(named, 1.0, 0.0)
        position = jnp.dot(
            jnp.broadcast_to(flag, (16, tokens)).astype(jnp.bfloat16), earlier, preferred_element_type=jnp.float32
        )[0:1, :]
        place = jnp.where(named, position, -1.0).astype(jnp.int32)
        slot = lax.broadcasted_iota(jnp.int32, (capacity, tokens), 0)
        hit = slot == place
        value = jnp.where(is_first, weight_one, weight_two)
        picks[k * capacity : (k + 1) * capacity, :] = jnp.where(hit, 1.0, 0.0).astype(jnp.bfloat16)
        scales[k * capacity : (k + 1) * capacity, :] = jnp.sum(jnp.where(hit, value, 0.0), axis=1, keepdims=True)


def pick_kernel(firsts, both, middle, picks, scales, *refs):
    halves = len(firsts)
    near, far, (mine, other) = refs[:halves], refs[halves:-2], refs[-2:]
    capacity = mine.shape[0]

    def step(k):
        rows = jnp.where(middle[0] == 1, near[k][...], far[k][...]) if both else near[k][...]
        value = jnp.dot(picks[...], rows, preferred_element_type=jnp.float32) * scales[...]
        mine[...] = value[:capacity].astype(jnp.bfloat16)
        other[...] = value[capacity:].astype(jnp.bfloat16)

    if halves == 1:
        step(0)
    else:
        late = pl.program_id(0) >= firsts[1]
        pl.when(jnp.logical_not(late))(functools.partial(step, 0))
        pl.when(late)(functools.partial(step, 1))


def base_kernel(turned, *refs):
    pieces, out = refs[:-1], refs[-1]
    rows = jnp.concatenate([p[...] for p in pieces], axis=0)
    out[...] = jnp.dot(turned[...], rows, preferred_element_type=jnp.float32)


def product_kernel(base, turned, mine, got, send, keep):
    half = send.shape[0]
    rows = jnp.concatenate([mine[...], got[...]], axis=0)
    total = base[...] + jnp.dot(turned[...], rows, preferred_element_type=jnp.float32)
    send[...] = total[:half].astype(jnp.bfloat16)
    keep[...] = total[half:].astype(jnp.bfloat16)


def back_kernel(count, order, *refs):
    pieces = refs[:count]
    weight, preact, out = refs[count], refs[count + 1], refs[-1]
    width = weight.shape[1]
    rows = jnp.concatenate([p[...] for p in pieces], axis=1)
    back = lax.dot_general(rows, weight[0], (((1,), (1,)), ((), ())), preferred_element_type=jnp.float32)
    gate = preact[0, 0, :, :width].astype(jnp.float32)
    up = preact[0, 0, :, width:].astype(jnp.float32)
    sig = jax.nn.sigmoid(gate)
    out[0, 0, :, :width] = (back * up * sig * (1.0 + gate * (1.0 - sig))).astype(jnp.bfloat16)
    out[0, 0, :, width:] = (back * (gate * sig)).astype(jnp.bfloat16)


def adam_kernel(kept, near, far, master, moment1, moment2, *refs):
    out_master, out_one, out_two, out_weight = refs[-4:]
    gradient = (kept[...].astype(jnp.float32) + near[...].astype(jnp.float32)) + far[...].astype(jnp.float32)
    moment_one = beta_first * moment1[0] + (1.0 - beta_first) * gradient
    moment_two = beta_second * moment2[0] + (1.0 - beta_second) * gradient * gradient
    step_size = (
        moment_one / bias_first / (jnp.sqrt(moment_two / bias_second) + adam_epsilon) + decay_rate * master[0]
    )
    master_next = master[0] - learn_rate * step_size
    out_master[0] = master_next
    out_one[0] = moment_one
    out_two[0] = moment_two
    out_weight[...] = master_next.astype(jnp.bfloat16)


def assemble_kernel(places, own, across, sibling, *refs):
    out = refs[-1]
    rows = own.shape[0]

    def put(g, value):
        out[0, pl.ds(pl.multiple_of(places[g] * rows, 16), rows), :] = value

    put(3, own[...])
    put(2, across[...])
    put(1, sibling[:rows, :])
    put(0, sibling[rows:, :])


def line_body(cotangent, routing, route_weight, saved_preact, weight, master, moment1, moment2):
    tokens, width = cotangent.shape[1:]
    slots, hidden_width = saved_preact.shape[2], weight.shape[1]
    capacity = slots // 8
    rows = hidden_width // 4
    expert = lax.axis_index("expert")
    replica = lax.axis_index("dp")
    z, y = expert // 2, expert % 2
    x, core = replica // 2, replica % 2
    middle = jnp.where((z == 1) | (z == 2), 1, 0).astype(jnp.int32).reshape(1)
    lower = z < 2
    blocks = [z, z ^ 1, jnp.where(lower, 2, 1), jnp.where(lower, 3, 0)]
    order = jnp.stack([b * 2 + s for b in blocks for s in (y, 1 - y)]).astype(jnp.int32)
    experts = jnp.stack([expert, expert ^ 1]).astype(jnp.int32)
    groups = jnp.stack([(1 - x) * 2 + 1 - core, x * 2 + 1 - core, (1 - x) * 2 + core, x * 2 + core]).astype(jnp.int32)

    swap_pair = [(e, e ^ 2) for e in range(8)]
    swap_middle = [(2, 4), (4, 2), (3, 5), (5, 3)]
    to_end = [(4, 6), (5, 7), (2, 0), (3, 1)]
    swap_y = [(e, e ^ 1) for e in range(8)]
    swap_x = [(d, d ^ 2) for d in range(4)]
    swap_core = [(d, d ^ 1) for d in range(4)]

    wide = HALF
    vmem = pl.BlockSpec(memory_space=pltpu.VMEM)
    packed = call(
        pack_kernel,
        "pack",
        (),
        (),
        (cotangent, routing[0].T, route_weight[0].T),
        [ANY, vmem, vmem],
        shape((tokens + 16, wide), jnp.bfloat16),
        ANY,
        scratch=[
            pltpu.VMEM((tokens + 16, wide), jnp.bfloat16),
            pltpu.SemaphoreType.DMA((8,)),
            pltpu.SemaphoreType.DMA((9,)),
        ],
        moved=4 * tokens * width,
        limit=PACK_LIMIT,
    )
    own = [packed, cotangent[0, :, wide:]]

    def permuted(parts, way):
        return [lax.ppermute(p, "expert", way) for p in parts]

    pair = permuted(own, swap_pair)
    middle_one = permuted(own, swap_middle)

    def tables(*given):
        spec = pl.BlockSpec((16, tokens), lambda i, m, e: (tokens // 16, 0))
        return call(
            table_kernel,
            "tables",
            (1,),
            (middle, experts),
            given,
            [spec] * len(given),
            (shape((2 * capacity, tokens), jnp.bfloat16), shape((2 * capacity, 1), jnp.float32)),
            (
                pl.BlockSpec((2 * capacity, tokens), lambda i, m, e: (0, 0)),
                pl.BlockSpec((2 * capacity, 1), lambda i, m, e: (0, 0)),
            ),
            moved=5 * capacity * tokens,
            flops=10 * capacity * tokens,
        )

    def pick(table, near, far, offset, columns, tile=TILE, claim=0, late=0):
        steps, start = columns // tile, offset // tile
        counts = [p.shape[1] // tile for p in near] if len(near) > 1 else [steps]
        firsts = [sum(counts[:h]) for h in range(len(counts))]
        specs = [
            pl.BlockSpec((2 * capacity, tokens), lambda i, m: (0, 0)),
            pl.BlockSpec((2 * capacity, 1), lambda i, m: (0, 0)),
        ]

        def place(h, i):
            return jnp.clip(i - firsts[h], 0, counts[h] - 1) if len(counts) > 1 else i

        for h in range(len(near)):
            if far:
                specs.append(pl.BlockSpec((tokens, tile), lambda i, m, h=h: (0, (start + place(h, i)) * m[0])))
            else:
                specs.append(pl.BlockSpec((tokens, tile), lambda i, m, h=h: (0, start + place(h, i))))
        for h in range(len(far)):
            specs.append(pl.BlockSpec((tokens, tile), lambda i, m, h=h: (0, (late // tile + place(h, i)) * (1 - m[0]))))
        out = shape((capacity, columns), jnp.bfloat16)
        mine, other = call(
            functools.partial(pick_kernel, firsts, bool(far)),
            "pick",
            (steps,),
            (middle,),
            (*table, *near, *far),
            specs,
            (out, out),
            (pl.BlockSpec((capacity, tile), lambda i, m: (0, i)),) * 2,
            flops=4 * capacity * tokens * columns + claim * COST,
            moved=4 * (tokens + capacity) * columns,
        )
        return mine, other, lax.ppermute(other, "expert", swap_y)

    def back(place, pieces, previous):
        specs = [pl.BlockSpec(p.shape, lambda i, o: (0, 0)) for p in pieces]
        specs += [
            pl.BlockSpec((1, hidden_width, width), lambda i, o: (0, 0, 0)),
            pl.BlockSpec((1, 1, capacity, 2 * hidden_width), lambda i, o: (0, 0, o[place], 0)),
        ]
        ins = [*pieces, weight, saved_preact]
        aliases = {}
        if previous is not None:
            aliases = {len(ins): 0}
            ins.append(previous)
            specs.append(ANY)
        return call(
            functools.partial(back_kernel, len(pieces)),
            "back",
            (1,),
            (order,),
            ins,
            specs,
            shape(saved_preact.shape, jnp.bfloat16),
            pl.BlockSpec((1, 1, capacity, 2 * hidden_width), lambda i, o: (0, 0, o[place], 0)),
            aliases=aliases,
            flops=2 * capacity * hidden_width * width,
            moved=hidden_width * width + 6 * capacity * hidden_width + 2 * capacity * width,
        )

    mine0, other0, got0 = pick(tables(own[0]), own, (), 0, width)
    turned = call(
        hidden_kernel,
        "hidden",
        (8,),
        (order, groups),
        (saved_preact,),
        [pl.BlockSpec((1, 1, capacity, 2 * hidden_width), lambda i, o, g: (0, 0, o[i], 0))],
        shape((hidden_width, slots), jnp.bfloat16),
        pl.BlockSpec((hidden_width, capacity), lambda i, o, g: (0, i)),
        scratch=[pltpu.VMEM((hidden_width, capacity), jnp.bfloat16)],
        moved=9 * slots * hidden_width,
        flops=40 * slots * hidden_width,
    )
    grad_preact = back(0, [mine0], None)
    pair[0], middle_one[0], grad_preact, turned = after(pair[0], middle_one[0], grad_preact, turned)
    middle_two = permuted(pair[:1], swap_middle)
    end_one = permuted(middle_one[:1], to_end)
    grad_preact = back(1, [got0], grad_preact)
    pair[1], middle_one[1], grad_preact = after(pair[1], middle_one[1], grad_preact)
    middle_two += permuted(pair[1:], swap_middle)
    end_one += permuted(middle_one[1:], to_end)
    mine1, other1, got1 = pick(tables(pair[0]), pair, (), 0, width)
    grad_preact = back(2, [mine1], grad_preact)
    middle_two[0], end_one[0], grad_preact, got1 = after(middle_two[0], end_one[0], grad_preact, got1)

    chunks = CHUNKS

    early = 6 * capacity

    def base_product(half, mine2, got2):
        columns = mine2.shape[1]
        start = half * wide // TILE
        full = pl.BlockSpec((capacity, TILE), lambda i: (0, start + i))
        part = pl.BlockSpec((capacity, TILE), lambda i: (0, i))
        return call(
            base_kernel,
            "base",
            (columns // TILE,),
            (),
            (turned, mine0, got0, mine1, got1, mine2, got2),
            [pl.BlockSpec((hidden_width, early), lambda i: (0, 0))] + [full] * 4 + [part] * 2,
            shape((hidden_width, columns), jnp.float32),
            pl.BlockSpec((hidden_width, TILE), lambda i: (0, i)),
            flops=2 * hidden_width * early * columns,
            moved=2 * (hidden_width * early + early * columns) + 4 * hidden_width * columns,
        )

    def to_ends(half):
        sent = []
        for offset, columns in SENT:
            if (offset >= wide) == half:
                inner = offset - wide * half
                count = tokens if offset else tokens + 16
                sent.append(lax.ppermute(middle_two[half][:count, inner : inner + columns], "expert", to_end))
        return sent

    ends = to_ends(0)
    table2 = tables(middle_one[0], end_one[0])
    mine2, other2, got2 = pick(table2, middle_one[:1], end_one[:1], 0, wide, wide // 2)
    mine2, got2 = [mine2], [got2]
    grad_preact = back(3, [got1], grad_preact)
    middle_two[1], end_one[1], grad_preact, other2 = after(middle_two[1], end_one[1], grad_preact, other2)
    ends += to_ends(1)
    mine2b, other2, got2b = pick(table2, middle_one[1:], end_one[1:], 0, width - wide, width - wide)
    mine2.append(mine2b)
    got2.append(got2b)
    grad_preact = back(4, mine2, grad_preact)
    bases = [base_product(0, mine2[0], got2[0])]
    ends[0], grad_preact, bases[0] = after(ends[0], grad_preact, bases[0])
    last_table = tables(middle_two[0], ends[0])

    def last_block(k, chunk, end_two):
        offset, columns = chunk
        half = offset >= wide
        inner = offset - wide * half
        late = offset - SENT[k][0]
        return pick(last_table, (middle_two[half],), (end_two,), inner, columns, claim=CLAIM, late=late)

    def product(chunk, mine3, got3):
        offset, columns = chunk
        side = int(offset >= wide)
        start = (offset - wide * side) // TILE
        half = shape((2 * rows, columns), jnp.bfloat16)
        part = pl.BlockSpec((capacity, TILE), lambda i: (0, i))
        return call(
            product_kernel,
            "product",
            (columns // TILE,),
            (),
            (bases[side], turned, mine3, got3),
            [
                pl.BlockSpec((hidden_width, TILE), lambda i: (0, start + i)),
                pl.BlockSpec((hidden_width, 2 * capacity), lambda i: (0, 3)),
                part,
                part,
            ],
            (half, half),
            (pl.BlockSpec((2 * rows, TILE), lambda i: (0, i)),) * 2,
            flops=4 * hidden_width * capacity * columns,
            moved=4 * hidden_width * capacity + 6 * hidden_width * columns,
        )

    def adam(chunk, keep, near, far, previous):
        offset, columns = chunk
        start = offset // TILE
        state = pl.BlockSpec((1, rows, TILE), lambda i: (0, 0, start + i))
        second = pl.BlockSpec((rows, TILE), lambda i: (1, i))
        whole = pl.BlockSpec((rows, TILE), lambda i: (0, i))
        out_state = shape(master.shape, jnp.float32)
        return call(
            adam_kernel,
            "adam",
            (columns // TILE,),
            (),
            (keep, near, far, master, moment1, moment2, *previous),
            [second, second, whole, state, state, state] + [ANY] * len(previous),
            (out_state, out_state, out_state, shape((rows, columns), jnp.bfloat16)),
            (state, state, state, whole),
            aliases={6 + k: k for k in range(len(previous))},
            flops=20 * rows * columns,
            moved=32 * rows * columns,
        )

    def assemble(chunk, fresh, crossed, sibling, last):
        offset, columns = chunk
        start = offset // TILE
        return call(
            assemble_kernel,
            "assemble",
            (columns // TILE,),
            (groups,),
            (fresh, crossed, sibling, *last),
            [
                pl.BlockSpec((rows, TILE), lambda i, g: (0, i)),
                pl.BlockSpec((rows, TILE), lambda i, g: (0, i)),
                pl.BlockSpec((2 * rows, TILE), lambda i, g: (0, i)),
            ]
            + [ANY] * len(last),
            shape((1, hidden_width, width), jnp.bfloat16),
            pl.BlockSpec((1, hidden_width, TILE), lambda i, g: (0, 0, start + i)),
            aliases={3: 0} if last else None,
            moved=16 * rows * columns,
        )

    states, next_weight = (), ()
    mines, gots, others3 = [], [], []
    sends, keeps, nears, acrosses, fars = {}, {}, {}, {}, {}
    freshes, crosseds, siblings = {}, {}, {}

    def tied(value, token):
        return value if token is None else after(value, token)[0]

    def sum_core(k, token):
        sends[k], keeps[k] = product(chunks[k], mines[k], tied(gots[k], token))
        nears[k] = lax.ppermute(sends[k], "dp", swap_core)
        return sends[k]

    def sum_x(k, token):
        near = tied(nears[k], token)
        acrosses[k] = (keeps[k][:rows].astype(jnp.float32) + near[:rows].astype(jnp.float32)).astype(jnp.bfloat16)
        nears[k] = near
        fars[k] = lax.ppermute(acrosses[k], "dp", swap_x)
        return acrosses[k]

    def update(k, token):
        nonlocal states
        *states, freshes[k] = adam(chunks[k], keeps[k], nears[k], tied(fars[k], token), states)
        crosseds[k] = lax.ppermute(freshes[k], "dp", swap_x)
        return freshes[k]

    def gather_core(k, token):
        crosseds[k] = tied(crosseds[k], token)
        both = jnp.concatenate([freshes[k], crosseds[k]], axis=0)
        siblings[k] = lax.ppermute(both, "dp", swap_core)
        return both

    def gathered(k, token):
        nonlocal next_weight
        next_weight = (assemble(chunks[k], freshes[k], crosseds[k], tied(siblings[k], token), next_weight),)
        return next_weight[0]

    def arrive(k, chunk):
        mine3, other3, got3 = last_block(k, chunks[chunk], ends[k])
        mines.append(mine3)
        gots.append(got3)
        return other3

    other = arrive(0, 0)
    got2[1], _ = after(got2[1], other)
    bases.append(base_product(1, mine2[1], got2[1]))
    sum_core(0, bases[1])
    if EARLY:
        across = sum_x(0, None)
        ends[1], across = after(ends[1], across)
    else:
        ends[1], send = after(ends[1], sends[0])
    other = arrive(1, 1)
    if not EARLY:
        other = sum_x(0, other)
    fresh = update(0, other)
    got2[1], fresh = after(got2[1], fresh)
    grad_preact = back(5, got2, grad_preact)
    sum_core(1, grad_preact)
    ends[2], send = after(ends[2], sends[1])
    across = sum_x(1, ends[2])
    ends[2], across = after(ends[2], across)
    arrive(2, 2)
    other = arrive(2, 3)
    both = gather_core(0, other)
    fresh = update(1, both)
    send = sum_core(2, fresh)
    send = sum_core(3, send)
    across = sum_x(2, send)
    across = sum_x(3, across)
    mines[0], _ = after(mines[0], across)
    grad_preact = back(6, mines, grad_preact)
    placed = gathered(0, grad_preact)
    fresh = update(2, placed)
    fresh = update(3, fresh)
    both = gather_core(1, fresh)
    gots[0], _ = after(gots[0], both)
    grad_preact = back(7, gots, grad_preact)
    placed = gathered(1, grad_preact)
    both = gather_core(2, placed)
    gather_core(3, both)
    gathered(2, None)
    gathered(3, None)
    return (grad_preact, next_weight[0], *states)


def body(cotangent, routing, route_weight, saved_preact, weight, master, moment1, moment2):
    n_expert = lax.axis_size("expert")
    tokens = cotangent[0]
    width = tokens.shape[1]
    slots = saved_preact.shape[2]
    hidden_width = weight.shape[1]
    capacity = slots // n_expert
    route_count = routing.shape[2]
    chosen = routing[0].reshape(-1)
    onehot = (chosen[:, None] == jnp.arange(n_expert, dtype=jnp.int32)[None, :]).astype(jnp.int32)
    earlier = jnp.cumsum(onehot, axis=0) - onehot
    position = jnp.sum(earlier * onehot, axis=1)
    target = chosen * capacity + position
    source_token = jnp.arange(chosen.shape[0], dtype=jnp.int32) // route_count
    token_table = jnp.zeros((slots,), jnp.int32).at[target].set(source_token)
    weight_table = jnp.zeros((slots,), jnp.float32).at[target].set(route_weight[0].reshape(-1))
    scaled = (tokens[token_table].astype(jnp.float32) * weight_table[:, None]).astype(jnp.bfloat16)
    arrived = lax.all_to_all(
        scaled.reshape(n_expert, capacity, width), "expert", split_axis=0, concat_axis=0, tiled=True
    )
    arrived = arrived.reshape(slots, width)
    preact = saved_preact[0, 0].astype(jnp.float32)
    gate_value = preact[:, :hidden_width]
    up_value = preact[:, hidden_width:]
    sigmoid_gate = jax.nn.sigmoid(gate_value)
    activated = gate_value * sigmoid_gate
    hidden = (activated * up_value).astype(jnp.bfloat16)
    back = lax.dot_general(
        arrived, weight[0], (((1,), (1,)), ((), ())), preferred_element_type=jnp.float32
    )
    grad_gate = back * up_value * sigmoid_gate * (1.0 + gate_value * (1.0 - sigmoid_gate))
    grad_up = back * activated
    grad_preact = jnp.concatenate([grad_gate, grad_up], axis=1).astype(jnp.bfloat16)[None, None]
    gradient = lax.psum_scatter(
        lax.dot_general(
            hidden, arrived, (((0,), (0,)), ((), ())), preferred_element_type=jnp.float32
        ).astype(jnp.bfloat16),
        "dp",
        scatter_dimension=0,
        tiled=True,
    ).astype(jnp.float32)
    moment_one = beta_first * moment1[0] + (1.0 - beta_first) * gradient
    moment_two = beta_second * moment2[0] + (1.0 - beta_second) * gradient * gradient
    step_size = (
        moment_one / bias_first / (jnp.sqrt(moment_two / bias_second) + adam_epsilon)
        + decay_rate * master[0]
    )
    master_next = master[0] - learn_rate * step_size
    weight_next = lax.all_gather(master_next.astype(jnp.bfloat16), "dp", axis=0, tiled=True)
    return (grad_preact, weight_next[None], master_next[None], moment_one[None], moment_two[None])


def solution(mesh):
    placed = (
        P("dp", "expert", None),
        P("dp", "expert", None),
        P("dp", "expert", None),
        P("dp", "expert", None, None),
        P("expert", None, None),
        P("expert", "dp", None),
        P("expert", "dp", None),
        P("expert", "dp", None),
    )
    line = mesh.shape["expert"] == 8 and mesh.shape["dp"] == 4
    return jax.shard_map(
        line_body if line else body,
        mesh=mesh,
        in_specs=placed,
        out_specs=(
            P("dp", "expert", None, None),
            P("expert", None, None),
            P("expert", "dp", None),
            P("expert", "dp", None),
            P("expert", "dp", None),
        ),
        check_vma=False,
    )
```

```python
import functools

import jax
import jax.numpy as jnp
from jax import lax
from jax.experimental import pallas as pl
from jax.experimental.pallas import tpu as pltpu
from jax.sharding import PartitionSpec as P

beta_first = 0.9
beta_second = 0.95
bias_first = 1.0 - 0.9**10
bias_second = 1.0 - 0.95**10
adam_epsilon = 1e-08
learn_rate = 0.001
decay_rate = 0.1

VMEM_LIMIT = 24 * 1024 * 1024
COST = 4096
EARLY = True
SUM = 2
CLAIM = (3_000_000_000, 3_000_000_000, 3_000_000_000)
TILE = 256
HALF = 1280
PACK_LIMIT = 56 * 1024 * 1024
SENT = ((0, 512), (512, 768), (1280, 768))
CHUNKS = ((0, 512), (512, 768), (1280, 512), (1792, 256))
ANY = pl.BlockSpec(memory_space=pl.ANY)


def params(limit):
    return pltpu.CompilerParams(vmem_limit_bytes=limit)


def call(kernel, name, grid, scalars, ins, specs, outs, out_specs, scratch=(), aliases=None, flops=0, moved=0, limit=VMEM_LIMIT):
    shift = len(scalars)
    return pl.pallas_call(
        kernel,
        name=name,
        grid_spec=pltpu.PrefetchScalarGridSpec(
            num_scalar_prefetch=shift,
            grid=grid,
            in_specs=specs,
            out_specs=out_specs,
            scratch_shapes=list(scratch),
        ),
        out_shape=outs,
        input_output_aliases={shift + a: b for a, b in (aliases or {}).items()},
        compiler_params=params(limit),
        cost_estimate=pl.CostEstimate(flops=flops // COST, bytes_accessed=moved // COST, transcendentals=0),
    )(*scalars, *ins)


def after(*values):
    return lax.optimization_barrier(values)


def shape(dims, dtype):
    return jax.ShapeDtypeStruct(dims, dtype)


def hidden_kernel(order, groups, preact, out, turned):
    width = preact.shape[-1] // 2
    gate = preact[0, 0, :, :width].astype(jnp.float32)
    up = preact[0, 0, :, width:].astype(jnp.float32)
    value = gate * jax.nn.sigmoid(gate) * up
    turned[...] = value.T.astype(jnp.bfloat16)
    rows = width // 4
    for g in range(4):
        start = pl.multiple_of(groups[g] * rows, 16)
        out[g * rows : (g + 1) * rows, :] = turned[pl.ds(start, rows), :]


def pack_kernel(tokens, chosen, weights, packed, held, into, out):
    count, wide = tokens.shape[1], packed.shape[1]
    parts = 8
    part = count // parts
    loads, stores = [], []
    for k in range(parts):
        here = pl.ds(k * part, part)
        loads.append(pltpu.make_async_copy(tokens.at[0, here, pl.ds(0, wide)], held.at[here, :], into.at[k]))
        stores.append(pltpu.make_async_copy(held.at[here, :], packed.at[here, :], out.at[k]))
    tail = pl.ds(count, 16)
    stores.append(pltpu.make_async_copy(held.at[tail, :], packed.at[tail, :], out.at[parts]))
    for load in loads:
        load.start()
    exact = weights[...]
    high = exact.astype(jnp.bfloat16).astype(jnp.float32)
    middle = (exact - high).astype(jnp.bfloat16).astype(jnp.float32)
    low = exact - high - middle
    info = jnp.concatenate([chosen[...].astype(jnp.float32), high, middle, low, jnp.zeros((8, count))], axis=0)
    held[count:, :] = jnp.zeros((16, wide), jnp.bfloat16)
    held[count:, :count] = info.astype(jnp.bfloat16)
    stores[parts].start()
    for k in range(parts):
        loads[k].wait()
        stores[k].start()
    for store in stores:
        store.wait()


def table_kernel(middle, experts, *refs):
    infos, picks, scales = refs[:-2], refs[-2], refs[-1]
    info = infos[0][...].astype(jnp.float32)
    if len(infos) == 2:
        info = jnp.where(middle[0] == 1, info, infos[1][...].astype(jnp.float32))
    capacity = picks.shape[0] // 2
    tokens = info.shape[1]
    first, second = info[0:1, :], info[1:2, :]
    weight_one = (info[2:3, :] + info[4:5, :]) + info[6:7, :]
    weight_two = (info[3:4, :] + info[5:6, :]) + info[7:8, :]
    before = lax.broadcasted_iota(jnp.int32, (tokens, tokens), 0)
    after = lax.broadcasted_iota(jnp.int32, (tokens, tokens), 1)
    earlier = (before < after).astype(jnp.float32).astype(jnp.bfloat16)
    for k in range(2):
        expert = experts[k].astype(jnp.float32)
        is_first = first == expert
        named = jnp.logical_or(is_first, second == expert)
        flag = jnp.where(named, 1.0, 0.0)
        position = jnp.dot(
            jnp.broadcast_to(flag, (16, tokens)).astype(jnp.bfloat16), earlier, preferred_element_type=jnp.float32
        )[0:1, :]
        place = jnp.where(named, position, -1.0).astype(jnp.int32)
        slot = lax.broadcasted_iota(jnp.int32, (capacity, tokens), 0)
        hit = slot == place
        value = jnp.where(is_first, weight_one, weight_two)
        picks[k * capacity : (k + 1) * capacity, :] = jnp.where(hit, 1.0, 0.0).astype(jnp.bfloat16)
        scales[k * capacity : (k + 1) * capacity, :] = jnp.sum(jnp.where(hit, value, 0.0), axis=1, keepdims=True)


def pick_kernel(firsts, both, middle, picks, scales, *refs):
    halves = len(firsts)
    near, far, (mine, other) = refs[:halves], refs[halves:-2], refs[-2:]
    capacity = mine.shape[0]

    def step(k):
        rows = jnp.where(middle[0] == 1, near[k][...], far[k][...]) if both else near[k][...]
        value = jnp.dot(picks[...], rows, preferred_element_type=jnp.float32) * scales[...]
        mine[...] = value[:capacity].astype(jnp.bfloat16)
        other[...] = value[capacity:].astype(jnp.bfloat16)

    if halves == 1:
        step(0)
    else:
        late = pl.program_id(0) >= firsts[1]
        pl.when(jnp.logical_not(late))(functools.partial(step, 0))
        pl.when(late)(functools.partial(step, 1))


def base_kernel(turned, *refs):
    pieces, out = refs[:-1], refs[-1]
    rows = jnp.concatenate([p[...] for p in pieces], axis=0)
    out[...] = jnp.dot(turned[...], rows, preferred_element_type=jnp.float32)


def product_kernel(base, turned, mine, got, *outs):
    *firsts, second, keep_first, keep_second = outs
    rows = jnp.concatenate([mine[...], got[...]], axis=0)
    total = base[...] + jnp.dot(turned[...], rows, preferred_element_type=jnp.float32)
    total = total.astype(jnp.bfloat16)
    quarter = second.shape[0]
    for k, out in enumerate((second, keep_first, keep_second), 1):
        out[...] = total[k * quarter : (k + 1) * quarter]
    for k, first in enumerate(firsts):

        @pl.when(pl.program_id(0) == k)
        def _():
            first[...] = total[:quarter]


def back_kernel(count, order, *refs):
    pieces = refs[:count]
    weight, preact, out = refs[count], refs[count + 1], refs[-1]
    width = weight.shape[1]
    rows = jnp.concatenate([p[...] for p in pieces], axis=1)
    back = lax.dot_general(rows, weight[0], (((1,), (1,)), ((), ())), preferred_element_type=jnp.float32)
    gate = preact[0, 0, :, :width].astype(jnp.float32)
    up = preact[0, 0, :, width:].astype(jnp.float32)
    sig = jax.nn.sigmoid(gate)
    out[0, 0, :, :width] = (back * up * sig * (1.0 + gate * (1.0 - sig))).astype(jnp.bfloat16)
    out[0, 0, :, width:] = (back * (gate * sig)).astype(jnp.bfloat16)


def adam_kernel(kept, near, far, master, moment1, moment2, *refs):
    out_master, out_one, out_two, out_weight = refs[-4:]
    gradient = (kept[...].astype(jnp.float32) + near[...].astype(jnp.float32)) + far[...].astype(jnp.float32)
    moment_one = beta_first * moment1[0] + (1.0 - beta_first) * gradient
    moment_two = beta_second * moment2[0] + (1.0 - beta_second) * gradient * gradient
    step_size = (
        moment_one / bias_first / (jnp.sqrt(moment_two / bias_second) + adam_epsilon) + decay_rate * master[0]
    )
    master_next = master[0] - learn_rate * step_size
    out_master[0] = master_next
    out_one[0] = moment_one
    out_two[0] = moment_two
    out_weight[...] = master_next.astype(jnp.bfloat16)


def assemble_kernel(places, own, across, sibling, *refs):
    out = refs[-1]
    rows = own.shape[0]

    def put(g, value):
        out[0, pl.ds(pl.multiple_of(places[g] * rows, 16), rows), :] = value

    put(3, own[...])
    put(2, across[...])
    put(1, sibling[:rows, :])
    put(0, sibling[rows:, :])


def line_body(cotangent, routing, route_weight, saved_preact, weight, master, moment1, moment2):
    tokens, width = cotangent.shape[1:]
    slots, hidden_width = saved_preact.shape[2], weight.shape[1]
    capacity = slots // 8
    rows = hidden_width // 4
    expert = lax.axis_index("expert")
    replica = lax.axis_index("dp")
    z, y = expert // 2, expert % 2
    x, core = replica // 2, replica % 2
    middle = jnp.where((z == 1) | (z == 2), 1, 0).astype(jnp.int32).reshape(1)
    lower = z < 2
    blocks = [z, z ^ 1, jnp.where(lower, 2, 1), jnp.where(lower, 3, 0)]
    order = jnp.stack([b * 2 + s for b in blocks for s in (y, 1 - y)]).astype(jnp.int32)
    experts = jnp.stack([expert, expert ^ 1]).astype(jnp.int32)
    groups = jnp.stack([(1 - x) * 2 + 1 - core, x * 2 + 1 - core, (1 - x) * 2 + core, x * 2 + core]).astype(jnp.int32)

    swap_pair = [(e, e ^ 2) for e in range(8)]
    swap_middle = [(2, 4), (4, 2), (3, 5), (5, 3)]
    to_end = [(4, 6), (5, 7), (2, 0), (3, 1)]
    swap_y = [(e, e ^ 1) for e in range(8)]
    swap_x = [(d, d ^ 2) for d in range(4)]
    swap_core = [(d, d ^ 1) for d in range(4)]

    wide = HALF
    vmem = pl.BlockSpec(memory_space=pltpu.VMEM)
    packed = call(
        pack_kernel,
        "pack",
        (),
        (),
        (cotangent, routing[0].T, route_weight[0].T),
        [ANY, vmem, vmem],
        shape((tokens + 16, wide), jnp.bfloat16),
        ANY,
        scratch=[
            pltpu.VMEM((tokens + 16, wide), jnp.bfloat16),
            pltpu.SemaphoreType.DMA((8,)),
            pltpu.SemaphoreType.DMA((9,)),
        ],
        moved=4 * tokens * width,
        limit=PACK_LIMIT,
    )
    own = [packed, cotangent[0, :, wide:]]

    def permuted(parts, way):
        return [lax.ppermute(p, "expert", way) for p in parts]

    pair = permuted(own, swap_pair)
    middle_one = permuted(own, swap_middle)

    def tables(*given):
        spec = pl.BlockSpec((16, tokens), lambda i, m, e: (tokens // 16, 0))
        return call(
            table_kernel,
            "tables",
            (1,),
            (middle, experts),
            given,
            [spec] * len(given),
            (shape((2 * capacity, tokens), jnp.bfloat16), shape((2 * capacity, 1), jnp.float32)),
            (
                pl.BlockSpec((2 * capacity, tokens), lambda i, m, e: (0, 0)),
                pl.BlockSpec((2 * capacity, 1), lambda i, m, e: (0, 0)),
            ),
            moved=5 * capacity * tokens,
            flops=10 * capacity * tokens,
        )

    def pick(table, near, far, offset, columns, tile=TILE, claim=0, late=0):
        steps, start = columns // tile, offset // tile
        counts = [p.shape[1] // tile for p in near] if len(near) > 1 else [steps]
        firsts = [sum(counts[:h]) for h in range(len(counts))]
        specs = [
            pl.BlockSpec((2 * capacity, tokens), lambda i, m: (0, 0)),
            pl.BlockSpec((2 * capacity, 1), lambda i, m: (0, 0)),
        ]

        def place(h, i):
            return jnp.clip(i - firsts[h], 0, counts[h] - 1) if len(counts) > 1 else i

        for h in range(len(near)):
            if far:
                specs.append(pl.BlockSpec((tokens, tile), lambda i, m, h=h: (0, (start + place(h, i)) * m[0])))
            else:
                specs.append(pl.BlockSpec((tokens, tile), lambda i, m, h=h: (0, start + place(h, i))))
        for h in range(len(far)):
            specs.append(pl.BlockSpec((tokens, tile), lambda i, m, h=h: (0, (late // tile + place(h, i)) * (1 - m[0]))))
        out = shape((capacity, columns), jnp.bfloat16)
        mine, other = call(
            functools.partial(pick_kernel, firsts, bool(far)),
            "pick",
            (steps,),
            (middle,),
            (*table, *near, *far),
            specs,
            (out, out),
            (pl.BlockSpec((capacity, tile), lambda i, m: (0, i)),) * 2,
            flops=4 * capacity * tokens * columns + claim * COST,
            moved=4 * (tokens + capacity) * columns,
        )
        return mine, other, lax.ppermute(other, "expert", swap_y)

    def back(place, pieces, previous):
        specs = [pl.BlockSpec(p.shape, lambda i, o: (0, 0)) for p in pieces]
        specs += [
            pl.BlockSpec((1, hidden_width, width), lambda i, o: (0, 0, 0)),
            pl.BlockSpec((1, 1, capacity, 2 * hidden_width), lambda i, o: (0, 0, o[place], 0)),
        ]
        ins = [*pieces, weight, saved_preact]
        aliases = {}
        if previous is not None:
            aliases = {len(ins): 0}
            ins.append(previous)
            specs.append(ANY)
        return call(
            functools.partial(back_kernel, len(pieces)),
            "back",
            (1,),
            (order,),
            ins,
            specs,
            shape(saved_preact.shape, jnp.bfloat16),
            pl.BlockSpec((1, 1, capacity, 2 * hidden_width), lambda i, o: (0, 0, o[place], 0)),
            aliases=aliases,
            flops=2 * capacity * hidden_width * width,
            moved=hidden_width * width + 6 * capacity * hidden_width + 2 * capacity * width,
        )

    mine0, other0, got0 = pick(tables(own[0]), own, (), 0, width)
    turned = call(
        hidden_kernel,
        "hidden",
        (8,),
        (order, groups),
        (saved_preact,),
        [pl.BlockSpec((1, 1, capacity, 2 * hidden_width), lambda i, o, g: (0, 0, o[i], 0))],
        shape((hidden_width, slots), jnp.bfloat16),
        pl.BlockSpec((hidden_width, capacity), lambda i, o, g: (0, i)),
        scratch=[pltpu.VMEM((hidden_width, capacity), jnp.bfloat16)],
        moved=9 * slots * hidden_width,
        flops=40 * slots * hidden_width,
    )
    grad_preact = back(0, [mine0], None)
    pair[0], middle_one[0], grad_preact, turned = after(pair[0], middle_one[0], grad_preact, turned)
    middle_two = permuted(pair[:1], swap_middle)
    end_one = permuted(middle_one[:1], to_end)
    grad_preact = back(1, [got0], grad_preact)
    pair[1], middle_one[1], grad_preact = after(pair[1], middle_one[1], grad_preact)
    middle_two += permuted(pair[1:], swap_middle)
    end_one += permuted(middle_one[1:], to_end)
    mine1, other1, got1 = pick(tables(pair[0]), pair, (), 0, width)
    grad_preact = back(2, [mine1], grad_preact)
    middle_two[0], end_one[0], grad_preact, got1 = after(middle_two[0], end_one[0], grad_preact, got1)

    chunks = CHUNKS

    early = 6 * capacity

    def base_product(half, mine2, got2):
        columns = mine2.shape[1]
        start = half * wide // TILE
        full = pl.BlockSpec((capacity, TILE), lambda i: (0, start + i))
        part = pl.BlockSpec((capacity, TILE), lambda i: (0, i))
        return call(
            base_kernel,
            "base",
            (columns // TILE,),
            (),
            (turned, mine0, got0, mine1, got1, mine2, got2),
            [pl.BlockSpec((hidden_width, early), lambda i: (0, 0))] + [full] * 4 + [part] * 2,
            shape((hidden_width, columns), jnp.float32),
            pl.BlockSpec((hidden_width, TILE), lambda i: (0, i)),
            flops=2 * hidden_width * early * columns,
            moved=2 * (hidden_width * early + early * columns) + 4 * hidden_width * columns,
        )

    def to_ends(half):
        sent = []
        for offset, columns in SENT:
            if (offset >= wide) == half:
                inner = offset - wide * half
                count = tokens if offset else tokens + 16
                sent.append(lax.ppermute(middle_two[half][:count, inner : inner + columns], "expert", to_end))
        return sent

    ends = to_ends(0)
    table2 = tables(middle_one[0], end_one[0])
    mine2, other2, got2 = pick(table2, middle_one[:1], end_one[:1], 0, wide, wide // 2)
    mine2, got2 = [mine2], [got2]
    grad_preact = back(3, [got1], grad_preact)
    middle_two[1], end_one[1], grad_preact, other2 = after(middle_two[1], end_one[1], grad_preact, other2)
    ends += to_ends(1)
    mine2b, other2, got2b = pick(table2, middle_one[1:], end_one[1:], 0, width - wide, width - wide)
    mine2.append(mine2b)
    got2.append(got2b)
    grad_preact = back(4, mine2, grad_preact)
    bases = [base_product(0, mine2[0], got2[0])]
    ends[0], grad_preact, bases[0] = after(ends[0], grad_preact, bases[0])
    last_table = tables(middle_two[0], ends[0])

    def last_block(k, chunk, end_two):
        offset, columns = chunk
        half = offset >= wide
        inner = offset - wide * half
        late = offset - SENT[k][0]
        return pick(last_table, (middle_two[half],), (end_two,), inner, columns, claim=CLAIM[k], late=late)

    def product(chunk, mine3, got3):
        offset, columns = chunk
        side = int(offset >= wide)
        start = (offset - wide * side) // TILE
        quarter = shape((rows, columns), jnp.bfloat16)
        part = pl.BlockSpec((capacity, TILE), lambda i: (0, i))
        return call(
            product_kernel,
            "product",
            (columns // TILE,),
            (),
            (bases[side], turned, mine3, got3),
            [
                pl.BlockSpec((hidden_width, TILE), lambda i: (0, start + i)),
                pl.BlockSpec((hidden_width, 2 * capacity), lambda i: (0, 3)),
                part,
                part,
            ],
            (shape((rows, TILE), jnp.bfloat16),) * (columns // TILE) + (quarter,) * 3,
            (pl.BlockSpec((rows, TILE), lambda i: (0, 0)),) * (columns // TILE)
            + (pl.BlockSpec((rows, TILE), lambda i: (0, i)),) * 3,
            flops=4 * hidden_width * capacity * columns,
            moved=4 * hidden_width * capacity + 6 * hidden_width * columns,
        )

    def adam(chunk, keep, near, far, previous):
        offset, columns = chunk
        start = offset // TILE
        state = pl.BlockSpec((1, rows, TILE), lambda i: (0, 0, start + i))
        whole = pl.BlockSpec((rows, TILE), lambda i: (0, i))
        out_state = shape(master.shape, jnp.float32)
        return call(
            adam_kernel,
            "adam",
            (columns // TILE,),
            (),
            (keep, near, far, master, moment1, moment2, *previous),
            [whole, whole, whole, state, state, state] + [ANY] * len(previous),
            (out_state, out_state, out_state, shape((rows, columns), jnp.bfloat16)),
            (state, state, state, whole),
            aliases={6 + k: k for k in range(len(previous))},
            flops=20 * rows * columns,
            moved=32 * rows * columns,
        )

    def assemble(chunk, fresh, crossed, sibling, last):
        offset, columns = chunk
        start = offset // TILE
        return call(
            assemble_kernel,
            "assemble",
            (columns // TILE,),
            (groups,),
            (fresh, crossed, sibling, *last),
            [
                pl.BlockSpec((rows, TILE), lambda i, g: (0, i)),
                pl.BlockSpec((rows, TILE), lambda i, g: (0, i)),
                pl.BlockSpec((2 * rows, TILE), lambda i, g: (0, i)),
            ]
            + [ANY] * len(last),
            shape((1, hidden_width, width), jnp.bfloat16),
            pl.BlockSpec((1, hidden_width, TILE), lambda i, g: (0, 0, start + i)),
            aliases={3: 0} if last else None,
            moved=16 * rows * columns,
        )

    states, next_weight = (), ()
    mines, gots, others3 = [], [], []
    sends, keeps, nears, acrosses, fars = {}, {}, {}, {}, {}
    freshes, crosseds, siblings = {}, {}, {}

    def tied(value, token):
        return value if token is None else after(value, token)[0]

    def sum_core(k, token):
        *firsts, second, keep_first, keep_second = product(chunks[k], mines[k], tied(gots[k], token))
        keeps[k] = [keep_first, keep_second]
        nears[k] = [[lax.ppermute(p, "dp", swap_core) for p in firsts], lax.ppermute(second, "dp", swap_core)]
        sends[k] = second
        return second

    def sum_x(k, token, others=()):
        for c in (k, *others):
            near = jnp.concatenate(nears[c][0], axis=1)
            acrosses[c] = (keeps[c][0].astype(jnp.float32) + near.astype(jnp.float32)).astype(jnp.bfloat16)
        if others:
            group = after(*(acrosses[c] for c in (k, *others)))
            for c, value in zip((k, *others), group):
                acrosses[c] = value
        for c in (k, *others):
            fars[c] = lax.ppermute(acrosses[c], "dp", swap_x)
        return acrosses[k]

    def update(k, token):
        nonlocal states
        *states, freshes[k] = adam(chunks[k], keeps[k][1], nears[k][1], tied(fars[k], token), states)
        return freshes[k]

    def gather_x(k, token):
        freshes[k] = tied(freshes[k], token)
        crosseds[k] = lax.ppermute(freshes[k], "dp", swap_x)

    def gather_core(k, token):
        crosseds[k] = tied(crosseds[k], token)
        both = jnp.concatenate([freshes[k], crosseds[k]], axis=0)
        siblings[k] = lax.ppermute(both, "dp", swap_core)
        return both

    def gathered(k, token):
        nonlocal next_weight
        next_weight = (assemble(chunks[k], freshes[k], crosseds[k], tied(siblings[k], token), next_weight),)
        return next_weight[0]

    def arrive(k, chunk):
        mine3, other3, got3 = last_block(k, chunks[chunk], ends[k])
        mines.append(mine3)
        gots.append(got3)
        return other3

    other = arrive(0, 0)
    got2[1], _ = after(got2[1], other)
    bases.append(base_product(1, mine2[1], got2[1]))
    sum_core(0, bases[1])
    if EARLY:
        across = sum_x(0, None)
        ends[1], across = after(ends[1], across)
    else:
        ends[1], send = after(ends[1], sends[0])
    other = arrive(1, 1)
    if not EARLY:
        other = sum_x(0, other)
    fresh = update(0, other)
    got2[1], fresh = after(got2[1], fresh)
    grad_preact = back(5, got2, grad_preact)
    sum_core(1, grad_preact)
    if SUM == 0:
        ends[2], nears[1][0][0] = after(ends[2], nears[1][0][0])
        sum_x(1, None)
        gather_x(0, None)
    else:
        gather_x(0, None)
        crosseds[0], nears[1][0][0] = after(crosseds[0], nears[1][0][0])
        sum_x(1, None)
    if SUM == 2:
        ends[2], acrosses[1] = after(ends[2], acrosses[1])
    arrive(2, 2)
    other = arrive(2, 3)
    grad_preact = back(6, mines, grad_preact)
    fars[1], grad_preact = after(fars[1], grad_preact)
    update(1, None)
    gots[2], gots[3], freshes[1] = after(gots[2], gots[3], freshes[1])
    gather_x(1, None)
    gather_core(0, None)
    sum_core(2, None)
    sum_core(3, None)
    grad_preact = back(7, gots, grad_preact)
    crosseds[1], nears[2][0][0], nears[3][0][0], grad_preact = after(
        crosseds[1], nears[2][0][0], nears[3][0][0], grad_preact
    )
    sum_x(2, None, (3,))
    gather_core(1, None)
    gathered(0, None)
    gathered(1, None)
    fars[2], nears[2][1], nears[3][1], next_weight = after(fars[2], nears[2][1], nears[3][1], next_weight[0])
    next_weight = (next_weight,)
    update(2, None)
    fars[3], freshes[2] = after(fars[3], freshes[2])
    gather_x(2, None)
    update(3, None)
    gather_x(3, None)
    gather_core(2, None)
    gather_core(3, None)
    gathered(2, None)
    gathered(3, None)
    return (grad_preact, next_weight[0], *states)


def body(cotangent, routing, route_weight, saved_preact, weight, master, moment1, moment2):
    n_expert = lax.axis_size("expert")
    tokens = cotangent[0]
    width = tokens.shape[1]
    slots = saved_preact.shape[2]
    hidden_width = weight.shape[1]
    capacity = slots // n_expert
    route_count = routing.shape[2]
    chosen = routing[0].reshape(-1)
    onehot = (chosen[:, None] == jnp.arange(n_expert, dtype=jnp.int32)[None, :]).astype(jnp.int32)
    earlier = jnp.cumsum(onehot, axis=0) - onehot
    position = jnp.sum(earlier * onehot, axis=1)
    target = chosen * capacity + position
    source_token = jnp.arange(chosen.shape[0], dtype=jnp.int32) // route_count
    token_table = jnp.zeros((slots,), jnp.int32).at[target].set(source_token)
    weight_table = jnp.zeros((slots,), jnp.float32).at[target].set(route_weight[0].reshape(-1))
    scaled = (tokens[token_table].astype(jnp.float32) * weight_table[:, None]).astype(jnp.bfloat16)
    arrived = lax.all_to_all(
        scaled.reshape(n_expert, capacity, width), "expert", split_axis=0, concat_axis=0, tiled=True
    )
    arrived = arrived.reshape(slots, width)
    preact = saved_preact[0, 0].astype(jnp.float32)
    gate_value = preact[:, :hidden_width]
    up_value = preact[:, hidden_width:]
    sigmoid_gate = jax.nn.sigmoid(gate_value)
    activated = gate_value * sigmoid_gate
    hidden = (activated * up_value).astype(jnp.bfloat16)
    back = lax.dot_general(
        arrived, weight[0], (((1,), (1,)), ((), ())), preferred_element_type=jnp.float32
    )
    grad_gate = back * up_value * sigmoid_gate * (1.0 + gate_value * (1.0 - sigmoid_gate))
    grad_up = back * activated
    grad_preact = jnp.concatenate([grad_gate, grad_up], axis=1).astype(jnp.bfloat16)[None, None]
    gradient = lax.psum_scatter(
        lax.dot_general(
            hidden, arrived, (((0,), (0,)), ((), ())), preferred_element_type=jnp.float32
        ).astype(jnp.bfloat16),
        "dp",
        scatter_dimension=0,
        tiled=True,
    ).astype(jnp.float32)
    moment_one = beta_first * moment1[0] + (1.0 - beta_first) * gradient
    moment_two = beta_second * moment2[0] + (1.0 - beta_second) * gradient * gradient
    step_size = (
        moment_one / bias_first / (jnp.sqrt(moment_two / bias_second) + adam_epsilon)
        + decay_rate * master[0]
    )
    master_next = master[0] - learn_rate * step_size
    weight_next = lax.all_gather(master_next.astype(jnp.bfloat16), "dp", axis=0, tiled=True)
    return (grad_preact, weight_next[None], master_next[None], moment_one[None], moment_two[None])


def solution(mesh):
    placed = (
        P("dp", "expert", None),
        P("dp", "expert", None),
        P("dp", "expert", None),
        P("dp", "expert", None, None),
        P("expert", None, None),
        P("expert", "dp", None),
        P("expert", "dp", None),
        P("expert", "dp", None),
    )
    line = mesh.shape["expert"] == 8 and mesh.shape["dp"] == 4
    return jax.shard_map(
        line_body if line else body,
        mesh=mesh,
        in_specs=placed,
        out_specs=(
            P("dp", "expert", None, None),
            P("expert", None, None),
            P("expert", "dp", None),
            P("expert", "dp", None),
            P("expert", "dp", None),
        ),
        check_vma=False,
    )
```

```python
import functools

import jax
import jax.numpy as jnp
from jax import lax
from jax.experimental import pallas as pl
from jax.experimental.pallas import tpu as pltpu
from jax.sharding import PartitionSpec as P

beta_first = 0.9
beta_second = 0.95
bias_first = 1.0 - 0.9**10
bias_second = 1.0 - 0.95**10
adam_epsilon = 1e-08
learn_rate = 0.001
decay_rate = 0.1

VMEM_LIMIT = 24 * 1024 * 1024
COST = 4096
EARLY = True
SUM = 2
CLAIM = (3_000_000_000, 3_000_000_000, 3_000_000_000)
TILE = 256
HALF = 1280
PACK_LIMIT = 56 * 1024 * 1024
SENT = ((0, 512), (512, 768), (1280, 768))
CHUNKS = ((0, 512), (512, 768), (1280, 512), (1792, 256))
ANY = pl.BlockSpec(memory_space=pl.ANY)


def params(limit):
    return pltpu.CompilerParams(vmem_limit_bytes=limit)


def call(kernel, name, grid, scalars, ins, specs, outs, out_specs, scratch=(), aliases=None, flops=0, moved=0, limit=VMEM_LIMIT):
    shift = len(scalars)
    return pl.pallas_call(
        kernel,
        name=name,
        grid_spec=pltpu.PrefetchScalarGridSpec(
            num_scalar_prefetch=shift,
            grid=grid,
            in_specs=specs,
            out_specs=out_specs,
            scratch_shapes=list(scratch),
        ),
        out_shape=outs,
        input_output_aliases={shift + a: b for a, b in (aliases or {}).items()},
        compiler_params=params(limit),
        cost_estimate=pl.CostEstimate(flops=flops // COST, bytes_accessed=moved // COST, transcendentals=0),
    )(*scalars, *ins)


def after(*values):
    return lax.optimization_barrier(values)


def shape(dims, dtype):
    return jax.ShapeDtypeStruct(dims, dtype)


def hidden_kernel(order, groups, preact, out, turned):
    width = preact.shape[-1] // 2
    gate = preact[0, 0, :, :width].astype(jnp.float32)
    up = preact[0, 0, :, width:].astype(jnp.float32)
    value = gate * jax.nn.sigmoid(gate) * up
    turned[...] = value.T.astype(jnp.bfloat16)
    rows = width // 4
    for g in range(4):
        start = pl.multiple_of(groups[g] * rows, 16)
        out[g * rows : (g + 1) * rows, :] = turned[pl.ds(start, rows), :]


def pack_kernel(tokens, chosen, weights, packed, held, into, out):
    count, wide = tokens.shape[1], packed.shape[1]
    parts = 8
    part = count // parts
    loads, stores = [], []
    for k in range(parts):
        here = pl.ds(k * part, part)
        loads.append(pltpu.make_async_copy(tokens.at[0, here, pl.ds(0, wide)], held.at[here, :], into.at[k]))
        stores.append(pltpu.make_async_copy(held.at[here, :], packed.at[here, :], out.at[k]))
    tail = pl.ds(count, 16)
    stores.append(pltpu.make_async_copy(held.at[tail, :], packed.at[tail, :], out.at[parts]))
    for load in loads:
        load.start()
    exact = weights[...]
    high = exact.astype(jnp.bfloat16).astype(jnp.float32)
    middle = (exact - high).astype(jnp.bfloat16).astype(jnp.float32)
    low = exact - high - middle
    info = jnp.concatenate([chosen[...].astype(jnp.float32), high, middle, low, jnp.zeros((8, count))], axis=0)
    held[count:, :] = jnp.zeros((16, wide), jnp.bfloat16)
    held[count:, :count] = info.astype(jnp.bfloat16)
    stores[parts].start()
    for k in range(parts):
        loads[k].wait()
        stores[k].start()
    for store in stores:
        store.wait()


def table_kernel(middle, experts, *refs):
    infos, picks, scales = refs[:-2], refs[-2], refs[-1]
    info = infos[0][...].astype(jnp.float32)
    if len(infos) == 2:
        info = jnp.where(middle[0] == 1, info, infos[1][...].astype(jnp.float32))
    capacity = picks.shape[0] // 2
    tokens = info.shape[1]
    first, second = info[0:1, :], info[1:2, :]
    weight_one = (info[2:3, :] + info[4:5, :]) + info[6:7, :]
    weight_two = (info[3:4, :] + info[5:6, :]) + info[7:8, :]
    before = lax.broadcasted_iota(jnp.int32, (tokens, tokens), 0)
    after = lax.broadcasted_iota(jnp.int32, (tokens, tokens), 1)
    earlier = (before < after).astype(jnp.float32).astype(jnp.bfloat16)
    for k in range(2):
        expert = experts[k].astype(jnp.float32)
        is_first = first == expert
        named = jnp.logical_or(is_first, second == expert)
        flag = jnp.where(named, 1.0, 0.0)
        position = jnp.dot(
            jnp.broadcast_to(flag, (16, tokens)).astype(jnp.bfloat16), earlier, preferred_element_type=jnp.float32
        )[0:1, :]
        place = jnp.where(named, position, -1.0).astype(jnp.int32)
        slot = lax.broadcasted_iota(jnp.int32, (capacity, tokens), 0)
        hit = slot == place
        value = jnp.where(is_first, weight_one, weight_two)
        picks[k * capacity : (k + 1) * capacity, :] = jnp.where(hit, 1.0, 0.0).astype(jnp.bfloat16)
        scales[k * capacity : (k + 1) * capacity, :] = jnp.sum(jnp.where(hit, value, 0.0), axis=1, keepdims=True)


def pick_kernel(firsts, both, middle, picks, scales, *refs):
    halves = len(firsts)
    near, far, (mine, other) = refs[:halves], refs[halves:-2], refs[-2:]
    capacity = mine.shape[0]

    def step(k):
        rows = jnp.where(middle[0] == 1, near[k][...], far[k][...]) if both else near[k][...]
        value = jnp.dot(picks[...], rows, preferred_element_type=jnp.float32) * scales[...]
        mine[...] = value[:capacity].astype(jnp.bfloat16)
        other[...] = value[capacity:].astype(jnp.bfloat16)

    if halves == 1:
        step(0)
    else:
        late = pl.program_id(0) >= firsts[1]
        pl.when(jnp.logical_not(late))(functools.partial(step, 0))
        pl.when(late)(functools.partial(step, 1))


def base_kernel(turned, *refs):
    pieces, out = refs[:-1], refs[-1]
    rows = jnp.concatenate([p[...] for p in pieces], axis=0)
    out[...] = jnp.dot(turned[...], rows, preferred_element_type=jnp.float32)


def product_kernel(base, turned, mine, got, *outs):
    *firsts, second, keep_first, keep_second = outs
    rows = jnp.concatenate([mine[...], got[...]], axis=0)
    total = base[...] + jnp.dot(turned[...], rows, preferred_element_type=jnp.float32)
    total = total.astype(jnp.bfloat16)
    quarter = second.shape[0]
    for k, out in enumerate((second, keep_first, keep_second), 1):
        out[...] = total[k * quarter : (k + 1) * quarter]
    for k, first in enumerate(firsts):

        @pl.when(pl.program_id(0) == k)
        def _():
            first[...] = total[:quarter]


def back_kernel(count, order, *refs):
    pieces = refs[:count]
    weight, preact, out = refs[count], refs[count + 1], refs[-1]
    width = weight.shape[1]
    rows = jnp.concatenate([p[...] for p in pieces], axis=1)
    back = lax.dot_general(rows, weight[0], (((1,), (1,)), ((), ())), preferred_element_type=jnp.float32)
    gate = preact[0, 0, :, :width].astype(jnp.float32)
    up = preact[0, 0, :, width:].astype(jnp.float32)
    sig = jax.nn.sigmoid(gate)
    out[0, 0, :, :width] = (back * up * sig * (1.0 + gate * (1.0 - sig))).astype(jnp.bfloat16)
    out[0, 0, :, width:] = (back * (gate * sig)).astype(jnp.bfloat16)


def adam_kernel(kept, near, far, master, moment1, moment2, *refs):
    out_master, out_one, out_two, out_weight = refs[-4:]
    gradient = (kept[...].astype(jnp.float32) + near[...].astype(jnp.float32)) + far[...].astype(jnp.float32)
    moment_one = beta_first * moment1[0] + (1.0 - beta_first) * gradient
    moment_two = beta_second * moment2[0] + (1.0 - beta_second) * gradient * gradient
    step_size = (
        moment_one / bias_first / (jnp.sqrt(moment_two / bias_second) + adam_epsilon) + decay_rate * master[0]
    )
    master_next = master[0] - learn_rate * step_size
    out_master[0] = master_next
    out_one[0] = moment_one
    out_two[0] = moment_two
    out_weight[...] = master_next.astype(jnp.bfloat16)


def assemble_kernel(places, own, across, sibling, *refs):
    out = refs[-1]
    rows = own.shape[0]

    def put(g, value):
        out[0, pl.ds(pl.multiple_of(places[g] * rows, 16), rows), :] = value

    put(3, own[...])
    put(2, across[...])
    put(1, sibling[:rows, :])
    put(0, sibling[rows:, :])


def assemble_last(places, *refs):
    out = refs[-1]
    late = pl.program_id(0) == pl.num_programs(0) - 1

    def put(own, across, sibling):
        rows = own.shape[0]
        for g, value in ((3, own[...]), (2, across[...]), (1, sibling[:rows, :]), (0, sibling[rows:, :])):
            out[0, pl.ds(pl.multiple_of(places[g] * rows, 16), rows), :] = value

    pl.when(jnp.logical_not(late))(lambda: put(*refs[:3]))
    pl.when(late)(lambda: put(*refs[3:6]))


def line_body(cotangent, routing, route_weight, saved_preact, weight, master, moment1, moment2):
    tokens, width = cotangent.shape[1:]
    slots, hidden_width = saved_preact.shape[2], weight.shape[1]
    capacity = slots // 8
    rows = hidden_width // 4
    expert = lax.axis_index("expert")
    replica = lax.axis_index("dp")
    z, y = expert // 2, expert % 2
    x, core = replica // 2, replica % 2
    middle = jnp.where((z == 1) | (z == 2), 1, 0).astype(jnp.int32).reshape(1)
    lower = z < 2
    blocks = [z, z ^ 1, jnp.where(lower, 2, 1), jnp.where(lower, 3, 0)]
    order = jnp.stack([b * 2 + s for b in blocks for s in (y, 1 - y)]).astype(jnp.int32)
    experts = jnp.stack([expert, expert ^ 1]).astype(jnp.int32)
    groups = jnp.stack([(1 - x) * 2 + 1 - core, x * 2 + 1 - core, (1 - x) * 2 + core, x * 2 + core]).astype(jnp.int32)

    swap_pair = [(e, e ^ 2) for e in range(8)]
    swap_middle = [(2, 4), (4, 2), (3, 5), (5, 3)]
    to_end = [(4, 6), (5, 7), (2, 0), (3, 1)]
    swap_y = [(e, e ^ 1) for e in range(8)]
    swap_x = [(d, d ^ 2) for d in range(4)]
    swap_core = [(d, d ^ 1) for d in range(4)]

    wide = HALF
    vmem = pl.BlockSpec(memory_space=pltpu.VMEM)
    packed = call(
        pack_kernel,
        "pack",
        (),
        (),
        (cotangent, routing[0].T, route_weight[0].T),
        [ANY, vmem, vmem],
        shape((tokens + 16, wide), jnp.bfloat16),
        ANY,
        scratch=[
            pltpu.VMEM((tokens + 16, wide), jnp.bfloat16),
            pltpu.SemaphoreType.DMA((8,)),
            pltpu.SemaphoreType.DMA((9,)),
        ],
        moved=4 * tokens * width,
        limit=PACK_LIMIT,
    )
    own = [packed, cotangent[0, :, wide:]]

    def permuted(parts, way):
        return [lax.ppermute(p, "expert", way) for p in parts]

    pair = permuted(own, swap_pair)
    middle_one = permuted(own, swap_middle)

    def tables(*given):
        spec = pl.BlockSpec((16, tokens), lambda i, m, e: (tokens // 16, 0))
        return call(
            table_kernel,
            "tables",
            (1,),
            (middle, experts),
            given,
            [spec] * len(given),
            (shape((2 * capacity, tokens), jnp.bfloat16), shape((2 * capacity, 1), jnp.float32)),
            (
                pl.BlockSpec((2 * capacity, tokens), lambda i, m, e: (0, 0)),
                pl.BlockSpec((2 * capacity, 1), lambda i, m, e: (0, 0)),
            ),
            moved=5 * capacity * tokens,
            flops=10 * capacity * tokens,
        )

    def pick(table, near, far, offset, columns, tile=TILE, claim=0, late=0):
        steps, start = columns // tile, offset // tile
        counts = [p.shape[1] // tile for p in near] if len(near) > 1 else [steps]
        firsts = [sum(counts[:h]) for h in range(len(counts))]
        specs = [
            pl.BlockSpec((2 * capacity, tokens), lambda i, m: (0, 0)),
            pl.BlockSpec((2 * capacity, 1), lambda i, m: (0, 0)),
        ]

        def place(h, i):
            return jnp.clip(i - firsts[h], 0, counts[h] - 1) if len(counts) > 1 else i

        for h in range(len(near)):
            if far:
                specs.append(pl.BlockSpec((tokens, tile), lambda i, m, h=h: (0, (start + place(h, i)) * m[0])))
            else:
                specs.append(pl.BlockSpec((tokens, tile), lambda i, m, h=h: (0, start + place(h, i))))
        for h in range(len(far)):
            specs.append(pl.BlockSpec((tokens, tile), lambda i, m, h=h: (0, (late // tile + place(h, i)) * (1 - m[0]))))
        out = shape((capacity, columns), jnp.bfloat16)
        mine, other = call(
            functools.partial(pick_kernel, firsts, bool(far)),
            "pick",
            (steps,),
            (middle,),
            (*table, *near, *far),
            specs,
            (out, out),
            (pl.BlockSpec((capacity, tile), lambda i, m: (0, i)),) * 2,
            flops=4 * capacity * tokens * columns + claim * COST,
            moved=4 * (tokens + capacity) * columns,
        )
        return mine, other, lax.ppermute(other, "expert", swap_y)

    def back(place, pieces, previous):
        specs = [pl.BlockSpec(p.shape, lambda i, o: (0, 0)) for p in pieces]
        specs += [
            pl.BlockSpec((1, hidden_width, width), lambda i, o: (0, 0, 0)),
            pl.BlockSpec((1, 1, capacity, 2 * hidden_width), lambda i, o: (0, 0, o[place], 0)),
        ]
        ins = [*pieces, weight, saved_preact]
        aliases = {}
        if previous is not None:
            aliases = {len(ins): 0}
            ins.append(previous)
            specs.append(ANY)
        return call(
            functools.partial(back_kernel, len(pieces)),
            "back",
            (1,),
            (order,),
            ins,
            specs,
            shape(saved_preact.shape, jnp.bfloat16),
            pl.BlockSpec((1, 1, capacity, 2 * hidden_width), lambda i, o: (0, 0, o[place], 0)),
            aliases=aliases,
            flops=2 * capacity * hidden_width * width,
            moved=hidden_width * width + 6 * capacity * hidden_width + 2 * capacity * width,
        )

    mine0, other0, got0 = pick(tables(own[0]), own, (), 0, width)
    turned = call(
        hidden_kernel,
        "hidden",
        (8,),
        (order, groups),
        (saved_preact,),
        [pl.BlockSpec((1, 1, capacity, 2 * hidden_width), lambda i, o, g: (0, 0, o[i], 0))],
        shape((hidden_width, slots), jnp.bfloat16),
        pl.BlockSpec((hidden_width, capacity), lambda i, o, g: (0, i)),
        scratch=[pltpu.VMEM((hidden_width, capacity), jnp.bfloat16)],
        moved=9 * slots * hidden_width,
        flops=40 * slots * hidden_width,
    )
    grad_preact = back(0, [mine0], None)
    pair[0], middle_one[0], grad_preact, turned = after(pair[0], middle_one[0], grad_preact, turned)
    middle_two = permuted(pair[:1], swap_middle)
    end_one = permuted(middle_one[:1], to_end)
    grad_preact = back(1, [got0], grad_preact)
    pair[1], middle_one[1], grad_preact = after(pair[1], middle_one[1], grad_preact)
    middle_two += permuted(pair[1:], swap_middle)
    end_one += permuted(middle_one[1:], to_end)
    mine1, other1, got1 = pick(tables(pair[0]), pair, (), 0, width)
    grad_preact = back(2, [mine1], grad_preact)
    middle_two[0], end_one[0], grad_preact, got1 = after(middle_two[0], end_one[0], grad_preact, got1)

    chunks = CHUNKS

    early = 6 * capacity

    def base_product(half, mine2, got2):
        columns = mine2.shape[1]
        start = half * wide // TILE
        full = pl.BlockSpec((capacity, TILE), lambda i: (0, start + i))
        part = pl.BlockSpec((capacity, TILE), lambda i: (0, i))
        return call(
            base_kernel,
            "base",
            (columns // TILE,),
            (),
            (turned, mine0, got0, mine1, got1, mine2, got2),
            [pl.BlockSpec((hidden_width, early), lambda i: (0, 0))] + [full] * 4 + [part] * 2,
            shape((hidden_width, columns), jnp.float32),
            pl.BlockSpec((hidden_width, TILE), lambda i: (0, i)),
            flops=2 * hidden_width * early * columns,
            moved=2 * (hidden_width * early + early * columns) + 4 * hidden_width * columns,
        )

    def to_ends(half):
        sent = []
        for offset, columns in SENT:
            if (offset >= wide) == half:
                inner = offset - wide * half
                count = tokens if offset else tokens + 16
                sent.append(lax.ppermute(middle_two[half][:count, inner : inner + columns], "expert", to_end))
        return sent

    ends = to_ends(0)
    table2 = tables(middle_one[0], end_one[0])
    mine2, other2, got2 = pick(table2, middle_one[:1], end_one[:1], 0, wide, wide // 2)
    mine2, got2 = [mine2], [got2]
    grad_preact = back(3, [got1], grad_preact)
    middle_two[1], end_one[1], grad_preact, other2 = after(middle_two[1], end_one[1], grad_preact, other2)
    ends += to_ends(1)
    mine2b, other2, got2b = pick(table2, middle_one[1:], end_one[1:], 0, width - wide, width - wide)
    mine2.append(mine2b)
    got2.append(got2b)
    grad_preact = back(4, mine2, grad_preact)
    bases = [base_product(0, mine2[0], got2[0])]
    ends[0], grad_preact, bases[0] = after(ends[0], grad_preact, bases[0])
    last_table = tables(middle_two[0], ends[0])

    def last_block(k, chunk, end_two):
        offset, columns = chunk
        half = offset >= wide
        inner = offset - wide * half
        late = offset - SENT[k][0]
        return pick(last_table, (middle_two[half],), (end_two,), inner, columns, claim=CLAIM[k], late=late)

    def product(chunk, mine3, got3):
        offset, columns = chunk
        side = int(offset >= wide)
        start = (offset - wide * side) // TILE
        quarter = shape((rows, columns), jnp.bfloat16)
        part = pl.BlockSpec((capacity, TILE), lambda i: (0, i))
        return call(
            product_kernel,
            "product",
            (columns // TILE,),
            (),
            (bases[side], turned, mine3, got3),
            [
                pl.BlockSpec((hidden_width, TILE), lambda i: (0, start + i)),
                pl.BlockSpec((hidden_width, 2 * capacity), lambda i: (0, 3)),
                part,
                part,
            ],
            (shape((rows, TILE), jnp.bfloat16),) * (columns // TILE) + (quarter,) * 3,
            (pl.BlockSpec((rows, TILE), lambda i: (0, 0)),) * (columns // TILE)
            + (pl.BlockSpec((rows, TILE), lambda i: (0, i)),) * 3,
            flops=4 * hidden_width * capacity * columns,
            moved=4 * hidden_width * capacity + 6 * hidden_width * columns,
        )

    def adam(chunk, keep, near, far, previous):
        offset, columns = chunk
        start = offset // TILE
        state = pl.BlockSpec((1, rows, TILE), lambda i: (0, 0, start + i))
        whole = pl.BlockSpec((rows, TILE), lambda i: (0, i))
        out_state = shape(master.shape, jnp.float32)
        return call(
            adam_kernel,
            "adam",
            (columns // TILE,),
            (),
            (keep, near, far, master, moment1, moment2, *previous),
            [whole, whole, whole, state, state, state] + [ANY] * len(previous),
            (out_state, out_state, out_state, shape((rows, columns), jnp.bfloat16)),
            (state, state, state, whole),
            aliases={6 + k: k for k in range(len(previous))},
            flops=20 * rows * columns,
            moved=32 * rows * columns,
        )

    def assemble(chunk, fresh, crossed, sibling, last):
        offset, columns = chunk
        start = offset // TILE
        return call(
            assemble_kernel,
            "assemble",
            (columns // TILE,),
            (groups,),
            (fresh, crossed, sibling, *last),
            [
                pl.BlockSpec((rows, TILE), lambda i, g: (0, i)),
                pl.BlockSpec((rows, TILE), lambda i, g: (0, i)),
                pl.BlockSpec((2 * rows, TILE), lambda i, g: (0, i)),
            ]
            + [ANY] * len(last),
            shape((1, hidden_width, width), jnp.bfloat16),
            pl.BlockSpec((1, hidden_width, TILE), lambda i, g: (0, 0, start + i)),
            aliases={3: 0} if last else None,
            moved=16 * rows * columns,
        )

    states, next_weight = (), ()
    mines, gots, others3 = [], [], []
    sends, keeps, nears, acrosses, fars = {}, {}, {}, {}, {}
    freshes, crosseds, siblings = {}, {}, {}

    def tied(value, token):
        return value if token is None else after(value, token)[0]

    def sum_core(k, token):
        *firsts, second, keep_first, keep_second = product(chunks[k], mines[k], tied(gots[k], token))
        keeps[k] = [keep_first, keep_second]
        nears[k] = [[lax.ppermute(p, "dp", swap_core) for p in firsts], lax.ppermute(second, "dp", swap_core)]
        sends[k] = second
        return second

    def sum_x(k, token, others=()):
        for c in (k, *others):
            near = jnp.concatenate(nears[c][0], axis=1)
            acrosses[c] = (keeps[c][0].astype(jnp.float32) + near.astype(jnp.float32)).astype(jnp.bfloat16)
        if others:
            group = after(*(acrosses[c] for c in (k, *others)))
            for c, value in zip((k, *others), group):
                acrosses[c] = value
        for c in (k, *others):
            fars[c] = lax.ppermute(acrosses[c], "dp", swap_x)
        return acrosses[k]

    def update(k, token):
        nonlocal states
        *states, freshes[k] = adam(chunks[k], keeps[k][1], nears[k][1], tied(fars[k], token), states)
        return freshes[k]

    def gather_x(k, token):
        freshes[k] = tied(freshes[k], token)
        crosseds[k] = lax.ppermute(freshes[k], "dp", swap_x)

    def gather_core(k, token):
        crosseds[k] = tied(crosseds[k], token)
        both = jnp.concatenate([freshes[k], crosseds[k]], axis=0)
        siblings[k] = lax.ppermute(both, "dp", swap_core)
        return both

    def gathered(k, token):
        nonlocal next_weight
        next_weight = (assemble(chunks[k], freshes[k], crosseds[k], tied(siblings[k], token), next_weight),)
        return next_weight[0]

    def arrive(k, chunk):
        mine3, other3, got3 = last_block(k, chunks[chunk], ends[k])
        mines.append(mine3)
        gots.append(got3)
        return other3

    other = arrive(0, 0)
    got2[1], _ = after(got2[1], other)
    bases.append(base_product(1, mine2[1], got2[1]))
    sum_core(0, bases[1])
    if EARLY:
        across = sum_x(0, None)
        ends[1], across = after(ends[1], across)
    else:
        ends[1], send = after(ends[1], sends[0])
    other = arrive(1, 1)
    if not EARLY:
        other = sum_x(0, other)
    fresh = update(0, other)
    got2[1], fresh = after(got2[1], fresh)
    grad_preact = back(5, got2, grad_preact)
    sum_core(1, grad_preact)
    if SUM == 0:
        ends[2], nears[1][0][0] = after(ends[2], nears[1][0][0])
        sum_x(1, None)
        gather_x(0, None)
    else:
        gather_x(0, None)
        crosseds[0], nears[1][0][0] = after(crosseds[0], nears[1][0][0])
        sum_x(1, None)
    if SUM == 2:
        ends[2], acrosses[1] = after(ends[2], acrosses[1])
    arrive(2, 2)
    other = arrive(2, 3)
    grad_preact = back(6, mines, grad_preact)
    fars[1], grad_preact = after(fars[1], grad_preact)
    update(1, None)
    gots[2], gots[3], freshes[1] = after(gots[2], gots[3], freshes[1])
    gather_x(1, None)
    gather_core(0, None)
    sum_core(2, None)
    sum_core(3, None)
    grad_preact = back(7, gots, grad_preact)
    crosseds[1], nears[2][0][0], nears[3][0][0], grad_preact = after(
        crosseds[1], nears[2][0][0], nears[3][0][0], grad_preact
    )
    sum_x(2, None, (3,))
    gather_core(1, None)
    gathered(0, None)
    gathered(1, None)
    fars[2], nears[2][1], nears[3][1], next_weight = after(fars[2], nears[2][1], nears[3][1], next_weight[0])
    next_weight = (next_weight,)
    update(2, None)
    fars[3], freshes[2] = after(fars[3], freshes[2])
    gather_x(2, None)
    update(3, None)
    gather_x(3, None)
    gather_core(2, None)
    gather_core(3, None)
    start, count = chunks[2][0] // TILE, chunks[2][1] // TILE
    early = lambda i, g: (0, jnp.minimum(i, count - 1))
    fixed = lambda i, g: (0, 0)
    sizes = (rows, rows, 2 * rows)
    last_weight = call(
        assemble_last,
        "assemble",
        (count + 1,),
        (groups,),
        (freshes[2], crosseds[2], siblings[2], freshes[3], crosseds[3], siblings[3], next_weight[0]),
        [pl.BlockSpec((n, TILE), early) for n in sizes] + [pl.BlockSpec((n, TILE), fixed) for n in sizes] + [ANY],
        shape((1, hidden_width, width), jnp.bfloat16),
        pl.BlockSpec((1, hidden_width, TILE), lambda i, g: (0, 0, start + i)),
        aliases={6: 0},
        moved=16 * rows * TILE * (count + 1),
    )
    next_weight = (last_weight,)
    return (grad_preact, next_weight[0], *states)


def body(cotangent, routing, route_weight, saved_preact, weight, master, moment1, moment2):
    n_expert = lax.axis_size("expert")
    tokens = cotangent[0]
    width = tokens.shape[1]
    slots = saved_preact.shape[2]
    hidden_width = weight.shape[1]
    capacity = slots // n_expert
    route_count = routing.shape[2]
    chosen = routing[0].reshape(-1)
    onehot = (chosen[:, None] == jnp.arange(n_expert, dtype=jnp.int32)[None, :]).astype(jnp.int32)
    earlier = jnp.cumsum(onehot, axis=0) - onehot
    position = jnp.sum(earlier * onehot, axis=1)
    target = chosen * capacity + position
    source_token = jnp.arange(chosen.shape[0], dtype=jnp.int32) // route_count
    token_table = jnp.zeros((slots,), jnp.int32).at[target].set(source_token)
    weight_table = jnp.zeros((slots,), jnp.float32).at[target].set(route_weight[0].reshape(-1))
    scaled = (tokens[token_table].astype(jnp.float32) * weight_table[:, None]).astype(jnp.bfloat16)
    arrived = lax.all_to_all(
        scaled.reshape(n_expert, capacity, width), "expert", split_axis=0, concat_axis=0, tiled=True
    )
    arrived = arrived.reshape(slots, width)
    preact = saved_preact[0, 0].astype(jnp.float32)
    gate_value = preact[:, :hidden_width]
    up_value = preact[:, hidden_width:]
    sigmoid_gate = jax.nn.sigmoid(gate_value)
    activated = gate_value * sigmoid_gate
    hidden = (activated * up_value).astype(jnp.bfloat16)
    back = lax.dot_general(
        arrived, weight[0], (((1,), (1,)), ((), ())), preferred_element_type=jnp.float32
    )
    grad_gate = back * up_value * sigmoid_gate * (1.0 + gate_value * (1.0 - sigmoid_gate))
    grad_up = back * activated
    grad_preact = jnp.concatenate([grad_gate, grad_up], axis=1).astype(jnp.bfloat16)[None, None]
    gradient = lax.psum_scatter(
        lax.dot_general(
            hidden, arrived, (((0,), (0,)), ((), ())), preferred_element_type=jnp.float32
        ).astype(jnp.bfloat16),
        "dp",
        scatter_dimension=0,
        tiled=True,
    ).astype(jnp.float32)
    moment_one = beta_first * moment1[0] + (1.0 - beta_first) * gradient
    moment_two = beta_second * moment2[0] + (1.0 - beta_second) * gradient * gradient
    step_size = (
        moment_one / bias_first / (jnp.sqrt(moment_two / bias_second) + adam_epsilon)
        + decay_rate * master[0]
    )
    master_next = master[0] - learn_rate * step_size
    weight_next = lax.all_gather(master_next.astype(jnp.bfloat16), "dp", axis=0, tiled=True)
    return (grad_preact, weight_next[None], master_next[None], moment_one[None], moment_two[None])


def solution(mesh):
    placed = (
        P("dp", "expert", None),
        P("dp", "expert", None),
        P("dp", "expert", None),
        P("dp", "expert", None, None),
        P("expert", None, None),
        P("expert", "dp", None),
        P("expert", "dp", None),
        P("expert", "dp", None),
    )
    line = mesh.shape["expert"] == 8 and mesh.shape["dp"] == 4
    return jax.shard_map(
        line_body if line else body,
        mesh=mesh,
        in_specs=placed,
        out_specs=(
            P("dp", "expert", None, None),
            P("expert", None, None),
            P("expert", "dp", None),
            P("expert", "dp", None),
            P("expert", "dp", None),
        ),
        check_vma=False,
    )
```
